256 devices in a mesh: coarse: 16 (over x_hi, y, core), fine: 16 (over x_lo, z).
Axes of the slice: x: 4 (x_hi: 2, x_lo: 2; x = x_hi * 2 + x_lo), y: 4, z: 8, core: 2. Of those that a mesh axis runs over, the one named last changes fastest.
Arguments:
- activations: bfloat16 [131072, 1280], P(('coarse', 'fine')), may hold values from -6 to 6
- targets: int32 [131072], P(('coarse', 'fine')), may hold values from 0 to 4
- inner_squeeze_weight: bfloat16 [1280, 640], replicated, may hold values from -0.15625 to 0.15625
- inner_filter_taps: bfloat16 [3, 640, 640], replicated, may hold values from -0.125 to 0.125
- inner_expand_weight: bfloat16 [640, 1280], replicated, may hold values from -0.25 to 0.25
- outer_squeeze_weight: bfloat16 [1280, 640], replicated, may hold values from -0.15625 to 0.15625
- outer_filter_taps: bfloat16 [3, 640, 640], replicated, may hold values from -0.125 to 0.125
- outer_expand_weight: bfloat16 [640, 1280], replicated, may hold values from -0.25 to 0.25
- decoder: bfloat16 [5, 1280], replicated, may hold values from -0.059814453 to 0.059814453
Outputs:
- input_gradient: bfloat16 [131072, 1280], P(('coarse', 'fine'))
- token_loss: float32 [131072], P(('coarse', 'fine'))
The draws below stay inside these ranges and needn't reach their ends.
All inputs are finite; a program needn't handle non-finite values.
Results may differ from the reference program's by a relative error of at most 0.015.
Values may be sent and summed in bfloat16 or wider, within the bound.
A program may use at most 64 MiB of HBM per device.

```python
import math
import jax
import jax.numpy as jnp
from jax import lax

D = 1280
BOT = 640
VOCAB = 5
TAPS = 3
SEQ = 131072
INNER_DILATION = 1024
OUTER_DILATION = 32768


def set_ends(result, stream_key, least, top_value):
    longest = result.shape.index(max(result.shape))
    spots = []
    for shift in (0, 1):
        where = [jax.random.randint(jax.random.fold_in(stream_key, axis), (), 0, length) for axis, length in enumerate(result.shape)]
        where[longest] = (where[longest] + shift) % result.shape[longest]
        spots.append(tuple(where))
    return result.at[spots[0]].set(least).at[spots[1]].set(top_value)


def block_levels(own_key, extent, cuts, low, high):
    level = 1.0
    for dim, parts in cuts:
        steps = jax.random.uniform(jax.random.fold_in(jax.random.fold_in(own_key, 6), dim), (parts,), jnp.float32, low / len(cuts), high / len(cuts))
        level = level * jnp.repeat(jnp.exp(steps), extent[dim] // parts).reshape((-1,) + (1,) * (len(extent) - 1 - dim))
    return level


def noise(own_key, dims, scale, limit, shards=(), held_as=jnp.bfloat16):
    values = scale * jax.random.normal(own_key, dims, jnp.float32)
    if shards:
        values = values * block_levels(own_key, dims, shards, -0.22, 0.18)
    return jnp.clip(values, -limit, limit).astype(held_as)


def setup_inputs(seed: int = 0) -> dict:
    key_list = jax.random.split(jax.random.key(seed), 10)
    return {
        "activations": noise(key_list[0], (SEQ, D), 1.0, 6.0, ((0, 256),)),
        "targets": set_ends(jax.random.randint(key_list[1], (SEQ,), 0, VOCAB), jax.random.fold_in(key_list[1], 1), 0, VOCAB - 1).astype(jnp.int32),
        "inner_squeeze_weight": noise(key_list[2], (D, BOT), D ** -0.5, 0.15625),
        "inner_filter_taps": noise(key_list[3], (TAPS, BOT, BOT), (TAPS * BOT) ** -0.5, 0.125),
        "inner_expand_weight": noise(key_list[4], (BOT, D), BOT ** -0.5, 0.25),
        "outer_squeeze_weight": noise(key_list[5], (D, BOT), D ** -0.5, 0.15625),
        "outer_filter_taps": noise(key_list[6], (TAPS, BOT, BOT), (TAPS * BOT) ** -0.5, 0.125),
        "outer_expand_weight": noise(key_list[7], (BOT, D), BOT ** -0.5, 0.25),
        "decoder": jnp.clip(jax.random.uniform(key_list[8], (VOCAB, D), jnp.float32, -0.059814453, 0.059814453), -0.059814453, 0.059814453).astype(jnp.bfloat16),
    }


eps = 1e-05

def norm_rows(values):
    average = lax.optimization_barrier(jnp.mean(values, axis=-1, keepdims=True))
    centred = values - average
    factor = lax.rsqrt(lax.optimization_barrier(jnp.mean(centred * centred, axis=-1, keepdims=True)) + eps)
    return (centred * factor, factor)

def norm_back(normal, factor, upward):
    first_term = upward - lax.optimization_barrier(jnp.mean(upward, axis=-1, keepdims=True))
    return (first_term - normal * lax.optimization_barrier(jnp.mean(upward * normal, axis=-1, keepdims=True))) * factor

def gelu_exact(inputs):
    return 0.5 * inputs * (1.0 + lax.erf(inputs * (1.0 / math.sqrt(2.0))))

def gelu_slope(inputs):
    return 0.5 * (1.0 + lax.erf(inputs * (1.0 / math.sqrt(2.0)))) + inputs * jnp.exp(-0.5 * inputs * inputs) * (1.0 / math.sqrt(2.0 * math.pi))

def product(leading, trailing):
    return jnp.dot(leading, trailing, preferred_element_type=jnp.float32)

def product_t(leading, trailing):
    return lax.dot_general(leading, trailing, (((1,), (1,)), ((), ())), preferred_element_type=jnp.float32)

def residual_block_forward(block_in, squeeze, taps, expand, dilation):
    normal_in, _ = norm_rows(block_in.astype(jnp.float32))
    entry_act = gelu_exact(normal_in).astype(jnp.bfloat16)
    squeezed = product(entry_act, squeeze)
    normal_mid, _ = norm_rows(squeezed)
    middle = gelu_exact(normal_mid).astype(jnp.bfloat16)
    conv_sum = product(jnp.roll(middle, dilation, 0), taps[0]) + product(middle, taps[1]) + product(jnp.roll(middle, -dilation, 0), taps[2])
    normal_conv, _ = norm_rows(conv_sum)
    closing = gelu_exact(normal_conv).astype(jnp.bfloat16)
    block_out = (block_in.astype(jnp.float32) + product(closing, expand)).astype(jnp.bfloat16)
    return (block_out, squeezed, conv_sum)

def residual_block_backward(block_in, squeezed, conv_sum, squeeze, taps, expand, dilation, gradient_result):
    dclosing = product_t(gradient_result.astype(jnp.bfloat16), expand)
    normal_conv, factor_conv = norm_rows(conv_sum)
    dconv = norm_back(normal_conv, factor_conv, gelu_slope(normal_conv) * dclosing).astype(jnp.bfloat16)
    dmiddle = product_t(jnp.roll(dconv, -dilation, 0), taps[0]) + product_t(dconv, taps[1]) + product_t(jnp.roll(dconv, dilation, 0), taps[2])
    normal_mid, factor_mid = norm_rows(squeezed)
    dsqueezed = norm_back(normal_mid, factor_mid, gelu_slope(normal_mid) * dmiddle).astype(jnp.bfloat16)
    dentry = product_t(dsqueezed, squeeze)
    normal_in, factor_in = norm_rows(block_in.astype(jnp.float32))
    return gradient_result + norm_back(normal_in, factor_in, gelu_slope(normal_in) * dentry)

def reference(activations, targets, inner_squeeze_weight, inner_filter_taps, inner_expand_weight, outer_squeeze_weight, outer_filter_taps, outer_expand_weight, decoder):
    outer_block_input, inner_bottleneck_rows, inner_convolved = residual_block_forward(activations, inner_squeeze_weight, inner_filter_taps, inner_expand_weight, INNER_DILATION)
    final_output, outer_bottleneck_rows, outer_convolved = residual_block_forward(outer_block_input, outer_squeeze_weight, outer_filter_taps, outer_expand_weight, OUTER_DILATION)
    normal_final, factor_final = norm_rows(final_output.astype(jnp.float32))
    normed = normal_final.astype(jnp.bfloat16)
    logits = product_t(normed, decoder)
    exponent = jnp.exp(logits)
    totals = lax.optimization_barrier(jnp.sum(exponent, axis=-1, keepdims=True))
    onehot = (targets[:, None] == jnp.arange(VOCAB, dtype=jnp.int32)[None, :]).astype(jnp.float32)
    token_loss = jnp.log(totals[:, 0]) - lax.optimization_barrier(jnp.sum(logits * onehot, axis=-1))
    dlogits = (32.0 * (exponent / totals - onehot)).astype(jnp.bfloat16)
    gradient_result = norm_back(normal_final, factor_final, product(dlogits, decoder))
    gradient_result = residual_block_backward(outer_block_input, outer_bottleneck_rows, outer_convolved, outer_squeeze_weight, outer_filter_taps, outer_expand_weight, OUTER_DILATION, gradient_result)
    gradient_result = residual_block_backward(activations, inner_bottleneck_rows, inner_convolved, inner_squeeze_weight, inner_filter_taps, inner_expand_weight, INNER_DILATION, gradient_result)
    return (gradient_result.astype(jnp.bfloat16), token_loss)
```

```python
import functools
import math

import jax
import jax.numpy as jnp
from jax import lax
from jax.experimental import pallas as pl
from jax.experimental.pallas import tpu as pltpu
from jax.sharding import PartitionSpec as P

MESH = pl.DeviceIdType.MESH
F32, BF16 = jnp.float32, jnp.bfloat16
EPS = 1e-05
ROWS, D, BOT, VOCAB = 512, 1280, 640, 5
CHUNKS = 4
CH = ROWS // CHUNKS
QUARTER = CH // 4
EXTRA = 128
WIDE = D + EXTRA
TILE = 16


def normed(values):
    centred = values - jnp.mean(values, axis=-1, keepdims=True)
    factor = lax.rsqrt(jnp.mean(centred * centred, axis=-1, keepdims=True) + EPS)
    return centred * factor, factor


def norm_back(normal, factor, upward):
    first = upward - jnp.mean(upward, axis=-1, keepdims=True)
    return (first - normal * jnp.mean(upward * normal, axis=-1, keepdims=True)) * factor


def gelu(s):
    return 0.5 * s * (1.0 + lax.erf(s * (1.0 / math.sqrt(2.0))))


def slope(s):
    return 0.5 * (1.0 + lax.erf(s * (1.0 / math.sqrt(2.0)))) + s * jnp.exp(-0.5 * s * s) * (
        1.0 / math.sqrt(2.0 * math.pi)
    )


def dot(a, b):
    return jnp.dot(a, b, preferred_element_type=F32)


def dot_t(a, b):
    return lax.dot_general(a, b, (((1,), (1,)), ((), ())), preferred_element_type=F32)


def tiles(body, unroll=4):
    def step(i, carry):
        body(pl.multiple_of(i * TILE, TILE))
        return carry

    lax.fori_loop(0, CH // TILE, step, 0, unroll=unroll)


def lanes(column):
    return jnp.broadcast_to(column, (column.shape[0], 128))


def kernel(
    x_hbm, targets, dec, sq_i_hbm, taps_i_hbm, ex_i_hbm, sq_o_hbm, taps_o_hbm, ex_o_hbm,
    out_hbm, loss_out,
    x, sq_i, taps_i, ex_i, sq_o, taps_o, ex_o,
    n_in, f_in, n_mid, f_mid, n_conv, f_conv, sl_in, sl_mid,
    mid, mid_behind, mid_ahead, dconv, dconv_behind, dconv_ahead,
    xo_send, xo, g_send, g,
    ent, wide, narrow, outs,
    o_n_in, o_f_in, o_n_mid, o_f_mid, o_n_conv, o_f_conv, o_grad, o_mid, o_dconv,
    w_sem, x_sem, own_sem, out_sem, halo_send, halo_recv, turn_send, turn_recv,
):
    c, f = lax.axis_index("coarse"), lax.axis_index("fine")
    shard = c * 16 + f
    mine = c // 4

    def inner_partner(way):
        other = lax.rem(shard + (2 if way == 0 else 254), 256)
        return (other // 16, lax.rem(other, 16))

    def outer_partner(i):
        return (lax.rem(c + 4 * i, 16), f)

    barrier = pltpu.get_barrier_semaphore()
    for partner in (inner_partner(0), inner_partner(1), outer_partner(1), outer_partner(2), outer_partner(3)):
        pl.semaphore_signal(barrier, inc=1, device_id=partner, device_id_type=MESH)

    def x_copy(k):
        rows = pl.ds(pl.multiple_of(k * CH, CH), CH)
        return pltpu.make_async_copy(x_hbm.at[rows], x.at[rows], x_sem.at[k])

    weights = [
        pltpu.make_async_copy(src, dst, w_sem.at[i])
        for i, (src, dst) in enumerate(
            (
                (sq_i_hbm, sq_i), (taps_i_hbm, taps_i), (ex_i_hbm, ex_i),
                (sq_o_hbm, sq_o), (taps_o_hbm, taps_o), (ex_o_hbm, ex_o),
            )
        )
    ]
    x_copy(0).start()
    weights[0].start()
    for k in range(1, CHUNKS):
        x_copy(k).start()
    for weight in weights[1:]:
        weight.start()

    def halo(stage, way, k, source, target):
        rows = pl.ds(pl.multiple_of(k * CH, CH), CH)
        return pltpu.make_async_remote_copy(
            src_ref=source.at[rows],
            dst_ref=target.at[rows],
            send_sem=halo_send.at[stage, way, k],
            recv_sem=halo_recv.at[stage, way, k],
            device_id=inner_partner(way),
            device_id_type=MESH,
        )

    def mid_halos(k):
        return halo(0, 0, k, mid, mid_behind), halo(0, 1, k, mid, mid_ahead)

    def dconv_halos(k):
        return halo(1, 0, k, dconv, dconv_behind), halo(1, 1, k, dconv, dconv_ahead)

    def quarter(k, which):
        return pl.ds(pl.multiple_of(k * CH + which * QUARTER, QUARTER), QUARTER)

    def turn(stage, i, k, source, target):
        theirs = lax.rem(mine + i, 4)
        return pltpu.make_async_remote_copy(
            src_ref=source.at[quarter(k, theirs)],
            dst_ref=target.at[quarter(k, mine)],
            send_sem=turn_send.at[stage, i, k],
            recv_sem=turn_recv.at[stage, i, k],
            device_id=outer_partner(i),
            device_id_type=MESH,
        )

    def turns(stage, k):
        source, target = ((xo_send, xo), (g_send, g))[stage]
        return [turn(stage, i, k, source, target) for i in (1, 2, 3)] + [
            pltpu.make_async_copy(source.at[quarter(k, mine)], target.at[quarter(k, mine)], own_sem.at[stage, k])
        ]

    def await_turns(stage, k):
        *remote, own = turns(stage, k)
        for copy in remote:
            copy.wait_recv()
        own.wait()

    def at(k, r, rows=TILE):
        return pl.ds(pl.multiple_of(k * CH + r, TILE), rows)

    def enter(k):
        x_copy(k).wait()

        def first(r):
            n, factor = normed(x[at(k, r), :].astype(F32))
            n_in[at(k, r), :] = n
            f_in[at(k, r), :] = lanes(factor)
            ent[pl.ds(r, TILE), :] = gelu(n).astype(BF16)

        tiles(first)
        narrow[...] = dot(ent[...], sq_i[...])

        def second(r):
            n, factor = normed(narrow[pl.ds(r, TILE), :])
            n_mid[at(k, r), :] = n
            f_mid[at(k, r), :] = lanes(factor)
            mid[at(k, r), :] = gelu(n).astype(BF16)

        tiles(second)
        for copy in mid_halos(k):
            copy.start()

    def prepare(k):
        classes = lax.broadcasted_iota(jnp.int32, (EXTRA, CH), 0)
        columns = (classes == targets[k]).astype(F32).astype(BF16)
        eye = (classes == lax.broadcasted_iota(jnp.int32, (EXTRA, CH), 1)).astype(F32).astype(BF16)
        xo_send[at(k, 0, CH), D:] = dot_t(eye, columns).astype(BF16)

        def first(r):
            sl_in[at(k, r), :] = slope(n_in[at(k, r), :])
            sl_mid[at(k, r), :] = slope(n_mid[at(k, r), :])

        tiles(first)

    def converse(k):
        for copy in mid_halos(k):
            copy.wait_recv()
        rows = at(k, 0, CH)
        narrow[...] = (
            dot(mid_behind[rows, :], taps_i[0]) + dot(mid[rows, :], taps_i[1]) + dot(mid_ahead[rows, :], taps_i[2])
        )

        def first(r):
            n, factor = normed(narrow[pl.ds(r, TILE), :])
            n_conv[at(k, r), :] = n
            f_conv[at(k, r), :] = lanes(factor)
            ent[pl.ds(r, TILE), :BOT] = gelu(n).astype(BF16)

        tiles(first)
        wide[...] = dot(ent[:, :BOT], ex_i[...])

        def second(r):
            xo_send[at(k, r), :D] = (x[at(k, r), :].astype(F32) + wide[pl.ds(r, TILE), :]).astype(BF16)

        tiles(second)
        for copy in turns(0, k):
            copy.start()

    def around(padded):
        padded[pl.ds(0, QUARTER), :] = padded[pl.ds(CH, QUARTER), :]
        padded[pl.ds(QUARTER + CH, QUARTER), :] = padded[pl.ds(QUARTER, QUARTER), :]
        return padded[pl.ds(0, CH), :], padded[pl.ds(QUARTER, CH), :], padded[pl.ds(2 * QUARTER, CH), :]

    def outer(k):
        await_turns(0, k)

        def first(r):
            n, factor = normed(xo[at(k, r), :D].astype(F32))
            o_n_in[pl.ds(r, TILE), :] = n
            o_f_in[pl.ds(r, TILE), :] = lanes(factor)
            ent[pl.ds(r, TILE), :] = gelu(n).astype(BF16)

        tiles(first)
        narrow[...] = dot(ent[...], sq_o[...])

        def second(r):
            n, factor = normed(narrow[pl.ds(r, TILE), :])
            o_n_mid[pl.ds(r, TILE), :] = n
            o_f_mid[pl.ds(r, TILE), :] = lanes(factor)
            o_mid[pl.ds(QUARTER + r, TILE), :] = gelu(n).astype(BF16)

        tiles(second)
        behind, own, ahead = around(o_mid)
        narrow[...] = dot(behind, taps_o[0]) + dot(own, taps_o[1]) + dot(ahead, taps_o[2])

        def third(r):
            n, factor = normed(narrow[pl.ds(r, TILE), :])
            o_n_conv[pl.ds(r, TILE), :] = n
            o_f_conv[pl.ds(r, TILE), :] = lanes(factor)
            ent[pl.ds(r, TILE), :BOT] = gelu(n).astype(BF16)

        tiles(third)
        wide[...] = dot(ent[:, :BOT], ex_o[...])

        def fourth(r):
            final = (xo[at(k, r), :D].astype(F32) + wide[pl.ds(r, TILE), :]).astype(BF16)
            n, factor = normed(final.astype(F32))
            o_grad[pl.ds(r, TILE), :] = n
            narrow[pl.ds(r, TILE), :128] = lanes(factor)
            ent[pl.ds(r, TILE), :] = n.astype(BF16)

        tiles(fourth)
        logits = dot_t(ent[...], dec[...])
        lane = lax.broadcasted_iota(jnp.int32, (CH, EXTRA), 1)
        onehot = xo[at(k, 0, CH), D:].astype(F32)
        exponent = jnp.where(lane < VOCAB, jnp.exp(logits), 0.0)
        totals = jnp.sum(exponent, axis=-1, keepdims=True)
        token_loss = jnp.log(totals) - jnp.sum(logits * onehot, axis=-1, keepdims=True)
        high = token_loss.astype(BF16).astype(F32)
        g_send[at(k, 0, CH), D:] = jnp.where(
            lane == 0, high, jnp.where(lane == 1, token_loss - high, 0.0)
        ).astype(BF16)
        dlogits = (32.0 * (exponent / totals - onehot)).astype(BF16)
        wide[...] = dot(dlogits, dec[...])

        def fifth(r):
            grad = norm_back(o_grad[pl.ds(r, TILE), :], narrow[pl.ds(r, TILE), 0:1], wide[pl.ds(r, TILE), :])
            o_grad[pl.ds(r, TILE), :] = grad
            ent[pl.ds(r, TILE), :] = grad.astype(BF16)

        tiles(fifth)
        narrow[...] = dot_t(ent[...], ex_o[...])

        def sixth(r):
            n = o_n_conv[pl.ds(r, TILE), :]
            upward = slope(n) * narrow[pl.ds(r, TILE), :]
            o_dconv[pl.ds(QUARTER + r, TILE), :] = norm_back(n, o_f_conv[pl.ds(r, TILE), 0:1], upward).astype(BF16)

        tiles(sixth)
        behind, own, ahead = around(o_dconv)
        narrow[...] = dot_t(ahead, taps_o[0]) + dot_t(own, taps_o[1]) + dot_t(behind, taps_o[2])

        def seventh(r):
            n = o_n_mid[pl.ds(r, TILE), :]
            upward = slope(n) * narrow[pl.ds(r, TILE), :]
            ent[pl.ds(r, TILE), :BOT] = norm_back(n, o_f_mid[pl.ds(r, TILE), 0:1], upward).astype(BF16)

        tiles(seventh)
        wide[...] = dot_t(ent[:, :BOT], sq_o[...])

        def eighth(r):
            n = o_n_in[pl.ds(r, TILE), :]
            upward = slope(n) * wide[pl.ds(r, TILE), :]
            back = norm_back(n, o_f_in[pl.ds(r, TILE), 0:1], upward)
            g_send[at(k, r), :D] = (o_grad[pl.ds(r, TILE), :] + back).astype(BF16)

        tiles(eighth)
        for copy in turns(1, k):
            copy.start()

    def turn_back(k):
        await_turns(1, k)
        narrow[...] = dot_t(g[at(k, 0, CH), :D], ex_i[...])

        def first(r):
            n = n_conv[at(k, r), :]
            upward = slope(n) * narrow[pl.ds(r, TILE), :]
            dconv[at(k, r), :] = norm_back(n, f_conv[at(k, r), 0:1], upward).astype(BF16)

        tiles(first)
        for copy in dconv_halos(k):
            copy.start()

    def out_copy(k):
        rows = pl.ds(pl.multiple_of(k * CH, CH), CH)
        return pltpu.make_async_copy(outs.at[rows], out_hbm.at[rows], out_sem.at[k])

    def leave(k):
        loss_out[k] = dot_t(jnp.ones((8, EXTRA), BF16), g[at(k, 0, CH), D:])
        for copy in dconv_halos(k):
            copy.wait_recv()
        rows = at(k, 0, CH)
        narrow[...] = (
            dot_t(dconv_ahead[rows, :], taps_i[0])
            + dot_t(dconv[rows, :], taps_i[1])
            + dot_t(dconv_behind[rows, :], taps_i[2])
        )

        def first(r):
            upward = sl_mid[at(k, r), :] * narrow[pl.ds(r, TILE), :]
            ent[pl.ds(r, TILE), :BOT] = norm_back(n_mid[at(k, r), :], f_mid[at(k, r), 0:1], upward).astype(BF16)

        tiles(first)
        wide[...] = dot_t(ent[:, :BOT], sq_i[...])

        def second(r):
            upward = sl_in[at(k, r), :] * wide[pl.ds(r, TILE), :]
            back = norm_back(n_in[at(k, r), :], f_in[at(k, r), 0:1], upward)
            outs[at(k, r), :] = (g[at(k, r), :D].astype(F32) + back).astype(BF16)

        tiles(second)
        out_copy(k).start()

    def loop(count, body):
        def step(k, carry):
            body(k)
            return carry

        lax.fori_loop(0, count, step, 0)

    pl.semaphore_wait(barrier, 5)
    weights[0].wait()
    loop(CHUNKS, enter)
    loop(CHUNKS, prepare)
    for weight in weights[1:]:
        weight.wait()

    def middle(s):
        @pl.when(s < CHUNKS)
        def _():
            converse(s)

        @pl.when(s >= 1)
        def _():
            turn_back(s - 1)

        @pl.when(s < CHUNKS)
        def _():
            outer(s)

    loop(CHUNKS + 1, middle)
    loop(CHUNKS, leave)

    def finish(k):
        for copy in mid_halos(k) + dconv_halos(k):
            copy.wait_send()
        for stage in (0, 1):
            for copy in turns(stage, k)[:3]:
                copy.wait_send()
        out_copy(k).wait()

    loop(CHUNKS, finish)


def on_device(activations, targets, sq_i, taps_i, ex_i, sq_o, taps_o, ex_o, decoder):
    anywhere = pl.BlockSpec(memory_space=pl.ANY)
    vmem = pl.BlockSpec(memory_space=pltpu.VMEM)
    decoder = jnp.pad(decoder, ((0, EXTRA - VOCAB), (0, 0)))
    targets = targets.reshape(CHUNKS, 1, CH)
    v = pltpu.VMEM
    dma = pltpu.SemaphoreType.DMA
    out, loss = pl.pallas_call(
        kernel,
        out_shape=(
            jax.ShapeDtypeStruct((ROWS, D), BF16),
            jax.ShapeDtypeStruct((CHUNKS, 8, CH), F32),
        ),
        in_specs=[anywhere, vmem, vmem] + [anywhere] * 6,
        out_specs=(anywhere, vmem),
        scratch_shapes=[
            v((ROWS, D), BF16),
            v((D, BOT), BF16), v((3, BOT, BOT), BF16), v((BOT, D), BF16),
            v((D, BOT), BF16), v((3, BOT, BOT), BF16), v((BOT, D), BF16),
            v((ROWS, D), F32), v((ROWS, 128), F32),
            v((ROWS, BOT), F32), v((ROWS, 128), F32),
            v((ROWS, BOT), F32), v((ROWS, 128), F32),
            v((ROWS, D), F32), v((ROWS, BOT), F32),
            v((ROWS, BOT), BF16), v((ROWS, BOT), BF16), v((ROWS, BOT), BF16),
            v((ROWS, BOT), BF16), v((ROWS, BOT), BF16), v((ROWS, BOT), BF16),
            v((ROWS, WIDE), BF16), v((ROWS, WIDE), BF16), v((ROWS, WIDE), BF16), v((ROWS, WIDE), BF16),
            v((CH, D), BF16), v((CH, D), F32), v((CH, BOT), F32), v((ROWS, D), BF16),
            v((CH, D), F32), v((CH, 128), F32), v((CH, BOT), F32), v((CH, 128), F32),
            v((CH, BOT), F32), v((CH, 128), F32), v((CH, D), F32),
            v((CH + 2 * QUARTER, BOT), BF16), v((CH + 2 * QUARTER, BOT), BF16),
            dma((6,)), dma((CHUNKS,)), dma((2, CHUNKS)), dma((CHUNKS,)),
            dma((2, 2, CHUNKS)), dma((2, 2, CHUNKS)), dma((2, 4, CHUNKS)), dma((2, 4, CHUNKS)),
        ],
        compiler_params=pltpu.CompilerParams(
            collective_id=0, has_side_effects=True, vmem_limit_bytes=56 * 1024 * 1024
        ),
    )(activations, targets, decoder, sq_i, taps_i, ex_i, sq_o, taps_o, ex_o)
    return out, loss[:, 0, :].reshape(ROWS)


def solution(mesh):
    rows = P(("coarse", "fine"))
    return jax.shard_map(
        on_device,
        mesh=mesh,
        in_specs=(P(("coarse", "fine"), None), rows, P(), P(), P(), P(), P(), P(), P()),
        out_specs=(P(("coarse", "fine"), None), rows),
        check_vma=False,
    )
```

```python
import functools
import math

import jax
import jax.numpy as jnp
from jax import lax
from jax.experimental import pallas as pl
from jax.experimental.pallas import tpu as pltpu
from jax.sharding import PartitionSpec as P

MESH = pl.DeviceIdType.MESH
F32, BF16 = jnp.float32, jnp.bfloat16
EPS = 1e-05
ROWS, D, BOT, VOCAB = 512, 1280, 640, 5
CHUNKS = 4
CH = ROWS // CHUNKS
QUARTER = CH // 4
EXTRA = 128
WIDE = D + EXTRA
TILE = 16


def normed(values):
    centred = values - jnp.mean(values, axis=-1, keepdims=True)
    factor = lax.rsqrt(jnp.mean(centred * centred, axis=-1, keepdims=True) + EPS)
    return centred * factor, factor


def norm_back(normal, factor, upward):
    first = upward - jnp.mean(upward, axis=-1, keepdims=True)
    return (first - normal * jnp.mean(upward * normal, axis=-1, keepdims=True)) * factor


def gelu(s):
    return 0.5 * s * (1.0 + lax.erf(s * (1.0 / math.sqrt(2.0))))


def slope(s):
    return 0.5 * (1.0 + lax.erf(s * (1.0 / math.sqrt(2.0)))) + s * jnp.exp(-0.5 * s * s) * (
        1.0 / math.sqrt(2.0 * math.pi)
    )


def dot(a, b):
    return jnp.dot(a, b, preferred_element_type=F32)


def dot_t(a, b):
    return lax.dot_general(a, b, (((1,), (1,)), ((), ())), preferred_element_type=F32)


def tiles(body, unroll=CH // TILE):
    def step(i, carry):
        body(pl.multiple_of(i * TILE, TILE))
        return carry

    lax.fori_loop(0, CH // TILE, step, 0, unroll=unroll)


def lanes(column):
    return jnp.broadcast_to(column, (column.shape[0], 128))


def kernel(
    x_hbm, targets, decoder, sq_i_hbm, taps_i_hbm, ex_i_hbm, sq_o_hbm, taps_o_hbm, ex_o_hbm,
    outs, loss_out,
    x, sq_i, taps_i, ex_i, sq_o, taps_o, ex_o,
    n_in, f_in, n_mid, f_mid, n_conv, f_conv, sl_in, sl_mid,
    mid, mid_behind, mid_ahead, dconv, dconv_behind, dconv_ahead,
    xo_send, xo, g_send, g,
    ent, wide, narrow,
    o_n_in, o_f_in, o_n_mid, o_f_mid, o_n_conv, o_f_conv, o_grad, o_mid, o_dconv, dec,
    w_sem, x_sem, own_sem, halo_send, halo_recv, turn_send, turn_recv,
):
    c, f = lax.axis_index("coarse"), lax.axis_index("fine")
    shard = c * 16 + f
    mine = c // 4

    def inner_partner(way):
        other = lax.rem(shard + (2 if way == 0 else 254), 256)
        return (other // 16, lax.rem(other, 16))

    def outer_partner(i):
        return (lax.rem(c + 4 * i, 16), f)

    barrier = pltpu.get_barrier_semaphore()
    for partner in (inner_partner(0), inner_partner(1), outer_partner(1), outer_partner(2), outer_partner(3)):
        pl.semaphore_signal(barrier, inc=1, device_id=partner, device_id_type=MESH)

    def x_copy(k):
        rows = pl.ds(pl.multiple_of(k * CH, CH), CH)
        return pltpu.make_async_copy(x_hbm.at[rows], x.at[rows], x_sem.at[k])

    weights = [
        pltpu.make_async_copy(src, dst, w_sem.at[i])
        for i, (src, dst) in enumerate(
            (
                (sq_i_hbm, sq_i), (taps_i_hbm, taps_i), (ex_i_hbm, ex_i),
                (sq_o_hbm, sq_o), (taps_o_hbm, taps_o), (ex_o_hbm, ex_o),
            )
        )
    ]
    x_copy(0).start()
    weights[0].start()
    for k in range(1, CHUNKS):
        x_copy(k).start()
    for weight in weights[1:]:
        weight.start()

    def halo(stage, way, k, source, target):
        rows = pl.ds(pl.multiple_of(k * CH, CH), CH)
        return pltpu.make_async_remote_copy(
            src_ref=source.at[rows],
            dst_ref=target.at[rows],
            send_sem=halo_send.at[stage, way, k],
            recv_sem=halo_recv.at[stage, way, k],
            device_id=inner_partner(way),
            device_id_type=MESH,
        )

    def mid_halos(k):
        return halo(0, 0, k, mid, mid_behind), halo(0, 1, k, mid, mid_ahead)

    def dconv_halos(k):
        return halo(1, 0, k, dconv, dconv_behind), halo(1, 1, k, dconv, dconv_ahead)

    def quarter(k, which):
        return pl.ds(pl.multiple_of(k * CH + which * QUARTER, QUARTER), QUARTER)

    def turn(stage, i, k, source, target):
        theirs = lax.rem(mine + i, 4)
        return pltpu.make_async_remote_copy(
            src_ref=source.at[quarter(k, theirs)],
            dst_ref=target.at[quarter(k, mine)],
            send_sem=turn_send.at[stage, i, k],
            recv_sem=turn_recv.at[stage, i, k],
            device_id=outer_partner(i),
            device_id_type=MESH,
        )

    def turns(stage, k):
        source, target = ((xo_send, xo), (g_send, g))[stage]
        return [turn(stage, i, k, source, target) for i in (1, 2, 3)] + [
            pltpu.make_async_copy(source.at[quarter(k, mine)], target.at[quarter(k, mine)], own_sem.at[stage, k])
        ]

    def await_turns(stage, k):
        *remote, own = turns(stage, k)
        for copy in remote:
            copy.wait_recv()
        own.wait()

    def at(k, r, rows=TILE):
        return pl.ds(pl.multiple_of(k * CH + r, TILE), rows)

    def enter(k):
        x_copy(k).wait()

        def first(r):
            n, factor = normed(x[at(k, r), :].astype(F32))
            n_in[at(k, r), :] = n
            f_in[at(k, r), :] = lanes(factor)
            ent[pl.ds(r, TILE), :] = gelu(n).astype(BF16)

        tiles(first)
        narrow[...] = dot(ent[...], sq_i[...])

        def second(r):
            n, factor = normed(narrow[pl.ds(r, TILE), :])
            n_mid[at(k, r), :] = n
            f_mid[at(k, r), :] = lanes(factor)
            mid[at(k, r), :] = gelu(n).astype(BF16)

        tiles(second)

        @pl.when(k < 1)
        def _():
            for copy in mid_halos(k):
                copy.start()

    def prepare(k):
        classes = lax.broadcasted_iota(jnp.int32, (EXTRA, CH), 0)
        columns = (classes == targets[k]).astype(F32).astype(BF16)
        eye = (classes == lax.broadcasted_iota(jnp.int32, (EXTRA, CH), 1)).astype(F32).astype(BF16)
        xo_send[at(k, 0, CH), D:] = dot_t(eye, columns).astype(BF16)

        def first(r):
            sl_in[at(k, r), :] = slope(n_in[at(k, r), :])
            sl_mid[at(k, r), :] = slope(n_mid[at(k, r), :])

        tiles(first)

    def converse(k):
        for copy in mid_halos(k):
            copy.wait_recv()

        @pl.when(k + 1 < CHUNKS)
        def _():
            for copy in mid_halos(k + 1):
                copy.start()

        rows = at(k, 0, CH)
        narrow[...] = (
            dot(mid_behind[rows, :], taps_i[0]) + dot(mid[rows, :], taps_i[1]) + dot(mid_ahead[rows, :], taps_i[2])
        )

        def first(r):
            n, factor = normed(narrow[pl.ds(r, TILE), :])
            n_conv[at(k, r), :] = n
            f_conv[at(k, r), :] = lanes(factor)
            ent[pl.ds(r, TILE), :BOT] = gelu(n).astype(BF16)

        tiles(first)
        wide[...] = dot(ent[:, :BOT], ex_i[...])

        def second(r):
            xo_send[at(k, r), :D] = (x[at(k, r), :].astype(F32) + wide[pl.ds(r, TILE), :]).astype(BF16)

        tiles(second)
        for copy in turns(0, k):
            copy.start()

    def around(padded):
        padded[pl.ds(0, QUARTER), :] = padded[pl.ds(CH, QUARTER), :]
        padded[pl.ds(QUARTER + CH, QUARTER), :] = padded[pl.ds(QUARTER, QUARTER), :]
        return padded[pl.ds(0, CH), :], padded[pl.ds(QUARTER, CH), :], padded[pl.ds(2 * QUARTER, CH), :]

    def outer(k):
        await_turns(0, k)

        def first(r):
            n, factor = normed(xo[at(k, r), :D].astype(F32))
            o_n_in[pl.ds(r, TILE), :] = n
            o_f_in[pl.ds(r, TILE), :] = lanes(factor)
            ent[pl.ds(r, TILE), :] = gelu(n).astype(BF16)

        tiles(first)
        narrow[...] = dot(ent[...], sq_o[...])

        def second(r):
            n, factor = normed(narrow[pl.ds(r, TILE), :])
            o_n_mid[pl.ds(r, TILE), :] = n
            o_f_mid[pl.ds(r, TILE), :] = lanes(factor)
            o_mid[pl.ds(QUARTER + r, TILE), :] = gelu(n).astype(BF16)

        tiles(second)
        behind, own, ahead = around(o_mid)
        narrow[...] = dot(behind, taps_o[0]) + dot(own, taps_o[1]) + dot(ahead, taps_o[2])

        def third(r):
            n, factor = normed(narrow[pl.ds(r, TILE), :])
            o_n_conv[pl.ds(r, TILE), :] = n
            o_f_conv[pl.ds(r, TILE), :] = lanes(factor)
            ent[pl.ds(r, TILE), :BOT] = gelu(n).astype(BF16)

        tiles(third)
        wide[...] = dot(ent[:, :BOT], ex_o[...])

        def fourth(r):
            final = (xo[at(k, r), :D].astype(F32) + wide[pl.ds(r, TILE), :]).astype(BF16)
            n, factor = normed(final.astype(F32))
            o_grad[pl.ds(r, TILE), :] = n
            narrow[pl.ds(r, TILE), :128] = lanes(factor)
            ent[pl.ds(r, TILE), :] = n.astype(BF16)

        tiles(fourth)
        logits = dot_t(ent[...], dec[...])
        lane = lax.broadcasted_iota(jnp.int32, (CH, EXTRA), 1)
        onehot = xo[at(k, 0, CH), D:].astype(F32)
        exponent = jnp.where(lane < VOCAB, jnp.exp(logits), 0.0)
        totals = jnp.sum(exponent, axis=-1, keepdims=True)
        token_loss = jnp.log(totals) - jnp.sum(logits * onehot, axis=-1, keepdims=True)
        high = token_loss.astype(BF16).astype(F32)
        g_send[at(k, 0, CH), D:] = jnp.where(
            lane == 0, high, jnp.where(lane == 1, token_loss - high, 0.0)
        ).astype(BF16)
        dlogits = (32.0 * (exponent / totals - onehot)).astype(BF16)
        wide[...] = dot(dlogits, dec[...])

        def fifth(r):
            grad = norm_back(o_grad[pl.ds(r, TILE), :], narrow[pl.ds(r, TILE), 0:1], wide[pl.ds(r, TILE), :])
            o_grad[pl.ds(r, TILE), :] = grad
            ent[pl.ds(r, TILE), :] = grad.astype(BF16)

        tiles(fifth)
        narrow[...] = dot_t(ent[...], ex_o[...])

        def sixth(r):
            n = o_n_conv[pl.ds(r, TILE), :]
            upward = slope(n) * narrow[pl.ds(r, TILE), :]
            o_dconv[pl.ds(QUARTER + r, TILE), :] = norm_back(n, o_f_conv[pl.ds(r, TILE), 0:1], upward).astype(BF16)

        tiles(sixth)
        behind, own, ahead = around(o_dconv)
        narrow[...] = dot_t(ahead, taps_o[0]) + dot_t(own, taps_o[1]) + dot_t(behind, taps_o[2])

        def seventh(r):
            n = o_n_mid[pl.ds(r, TILE), :]
            upward = slope(n) * narrow[pl.ds(r, TILE), :]
            ent[pl.ds(r, TILE), :BOT] = norm_back(n, o_f_mid[pl.ds(r, TILE), 0:1], upward).astype(BF16)

        tiles(seventh)
        wide[...] = dot_t(ent[:, :BOT], sq_o[...])

        def eighth(r):
            n = o_n_in[pl.ds(r, TILE), :]
            upward = slope(n) * wide[pl.ds(r, TILE), :]
            back = norm_back(n, o_f_in[pl.ds(r, TILE), 0:1], upward)
            g_send[at(k, r), :D] = (o_grad[pl.ds(r, TILE), :] + back).astype(BF16)

        tiles(eighth)
        for copy in turns(1, k):
            copy.start()

    def turn_back(k):
        await_turns(1, k)
        narrow[...] = dot_t(g[at(k, 0, CH), :D], ex_i[...])

        def first(r):
            n = n_conv[at(k, r), :]
            upward = slope(n) * narrow[pl.ds(r, TILE), :]
            dconv[at(k, r), :] = norm_back(n, f_conv[at(k, r), 0:1], upward).astype(BF16)

        tiles(first)
        for copy in dconv_halos(k):
            copy.start()

    def leave(k):
        loss_out[k] = dot_t(jnp.ones((8, EXTRA), BF16), g[at(k, 0, CH), D:])[0:1]
        for copy in dconv_halos(k):
            copy.wait_recv()
        rows = at(k, 0, CH)
        narrow[...] = (
            dot_t(dconv_ahead[rows, :], taps_i[0])
            + dot_t(dconv[rows, :], taps_i[1])
            + dot_t(dconv_behind[rows, :], taps_i[2])
        )

        def first(r):
            upward = sl_mid[at(k, r), :] * narrow[pl.ds(r, TILE), :]
            ent[pl.ds(r, TILE), :BOT] = norm_back(n_mid[at(k, r), :], f_mid[at(k, r), 0:1], upward).astype(BF16)

        tiles(first)
        wide[...] = dot_t(ent[:, :BOT], sq_i[...])

        def second(r):
            upward = sl_in[at(k, r), :] * wide[pl.ds(r, TILE), :]
            back = norm_back(n_in[at(k, r), :], f_in[at(k, r), 0:1], upward)
            outs[at(k, r), :] = (g[at(k, r), :D].astype(F32) + back).astype(BF16)

        tiles(second)

    def loop(count, body):
        def step(k, carry):
            body(k)
            return carry

        lax.fori_loop(0, count, step, 0)

    dec[...] = jnp.zeros_like(dec)
    dec[pl.ds(0, VOCAB), :] = decoder[...]
    pl.semaphore_wait(barrier, 5)
    weights[0].wait()
    loop(CHUNKS, enter)
    loop(CHUNKS, prepare)
    for weight in weights[1:]:
        weight.wait()

    def middle(step):
        s = step - 1

        @pl.when(s + 1 < CHUNKS)
        def _():
            converse(s + 1)

        @pl.when(jnp.logical_and(s >= 0, s < CHUNKS))
        def _():
            outer(s)

        @pl.when(s >= 1)
        def _():
            turn_back(s - 1)

    loop(CHUNKS + 2, middle)
    loop(CHUNKS, leave)

    def finish(k):
        for copy in mid_halos(k) + dconv_halos(k):
            copy.wait_send()
        for stage in (0, 1):
            for copy in turns(stage, k)[:3]:
                copy.wait_send()

    loop(CHUNKS, finish)


def on_device(activations, targets, sq_i, taps_i, ex_i, sq_o, taps_o, ex_o, decoder):
    anywhere = pl.BlockSpec(memory_space=pltpu.HBM)
    vmem = pl.BlockSpec(memory_space=pltpu.VMEM)
    targets = targets.reshape(CHUNKS, 1, CH)
    v = pltpu.VMEM
    dma = pltpu.SemaphoreType.DMA
    out, loss = pl.pallas_call(
        kernel,
        out_shape=(
            jax.ShapeDtypeStruct((ROWS, D), BF16),
            jax.ShapeDtypeStruct((CHUNKS, 1, CH), F32),
        ),
        in_specs=[anywhere, vmem, vmem] + [anywhere] * 6,
        out_specs=(vmem, vmem),
        scratch_shapes=[
            v((ROWS, D), BF16),
            v((D, BOT), BF16), v((3, BOT, BOT), BF16), v((BOT, D), BF16),
            v((D, BOT), BF16), v((3, BOT, BOT), BF16), v((BOT, D), BF16),
            v((ROWS, D), F32), v((ROWS, 128), F32),
            v((ROWS, BOT), F32), v((ROWS, 128), F32),
            v((ROWS, BOT), F32), v((ROWS, 128), F32),
            v((ROWS, D), F32), v((ROWS, BOT), F32),
            v((ROWS, BOT), BF16), v((ROWS, BOT), BF16), v((ROWS, BOT), BF16),
            v((ROWS, BOT), BF16), v((ROWS, BOT), BF16), v((ROWS, BOT), BF16),
            v((ROWS, WIDE), BF16), v((ROWS, WIDE), BF16), v((ROWS, WIDE), BF16), v((ROWS, WIDE), BF16),
            v((CH, D), BF16), v((CH, D), F32), v((CH, BOT), F32),
            v((CH, D), F32), v((CH, 128), F32), v((CH, BOT), F32), v((CH, 128), F32),
            v((CH, BOT), F32), v((CH, 128), F32), v((CH, D), F32),
            v((CH + 2 * QUARTER, BOT), BF16), v((CH + 2 * QUARTER, BOT), BF16), v((EXTRA, D), BF16),
            dma((6,)), dma((CHUNKS,)), dma((2, CHUNKS)),
            dma((2, 2, CHUNKS)), dma((2, 2, CHUNKS)), dma((2, 4, CHUNKS)), dma((2, 4, CHUNKS)),
        ],
        compiler_params=pltpu.CompilerParams(
            collective_id=0, has_side_effects=True, vmem_limit_bytes=62 * 1024 * 1024
        ),
    )(activations, targets, decoder, sq_i, taps_i, ex_i, sq_o, taps_o, ex_o)
    return out, loss.reshape(ROWS)


def solution(mesh):
    rows = P(("coarse", "fine"))
    return jax.shard_map(
        on_device,
        mesh=mesh,
        in_specs=(P(("coarse", "fine"), None), rows, P(), P(), P(), P(), P(), P(), P()),
        out_specs=(P(("coarse", "fine"), None), rows),
        check_vma=False,
    )
```

```python
import functools
import math

import jax
import jax.numpy as jnp
from jax import lax
from jax.experimental import pallas as pl
from jax.experimental.pallas import tpu as pltpu
from jax.sharding import PartitionSpec as P

MESH = pl.DeviceIdType.MESH
F32, BF16 = jnp.float32, jnp.bfloat16
EPS = 1e-05
ROWS, D, BOT, VOCAB = 512, 1280, 640, 5
CHUNKS = 4
CH = ROWS // CHUNKS
QUARTER = CH // 4
EXTRA = 128
WIDE = D + EXTRA
TILE = 16


def normed(values):
    centred = values - jnp.mean(values, axis=-1, keepdims=True)
    factor = lax.rsqrt(jnp.mean(centred * centred, axis=-1, keepdims=True) + EPS)
    return centred * factor, factor


def norm_back(normal, factor, upward):
    first = upward - jnp.mean(upward, axis=-1, keepdims=True)
    return (first - normal * jnp.mean(upward * normal, axis=-1, keepdims=True)) * factor


def gelu(s):
    return 0.5 * s * (1.0 + lax.erf(s * (1.0 / math.sqrt(2.0))))


def slope(s):
    return 0.5 * (1.0 + lax.erf(s * (1.0 / math.sqrt(2.0)))) + s * jnp.exp(-0.5 * s * s) * (
        1.0 / math.sqrt(2.0 * math.pi)
    )


def dot(a, b):
    return jnp.dot(a, b, preferred_element_type=F32)


def dot_t(a, b):
    return lax.dot_general(a, b, (((1,), (1,)), ((), ())), preferred_element_type=F32)


def tiles(body, unroll=CH // TILE):
    def step(i, carry):
        body(pl.multiple_of(i * TILE, TILE))
        return carry

    lax.fori_loop(0, CH // TILE, step, 0, unroll=unroll)


def lanes(column):
    return jnp.broadcast_to(column, (column.shape[0], 128))


def kernel(
    x_hbm, targets, decoder, sq_i_hbm, taps_i_hbm, ex_i_hbm, sq_o_hbm, taps_o_hbm, ex_o_hbm,
    outs, loss_out,
    x, sq_i, taps_i, ex_i, sq_o, taps_o, ex_o,
    n_in, f_in, n_mid, f_mid, n_conv, f_conv, sl_in, sl_mid,
    mid, mid_behind, mid_ahead, dconv, dconv_behind, dconv_ahead,
    xo_send, xo, g_send, g,
    ent, wide, narrow,
    o_n_in, o_f_in, o_n_mid, o_f_mid, o_n_conv, o_f_conv, o_grad, o_mid, o_dconv, dec,
    w_sem, x_sem, own_sem, halo_send, halo_recv, turn_send, turn_recv,
):
    c, f = lax.axis_index("coarse"), lax.axis_index("fine")
    shard = c * 16 + f
    mine = c // 4

    def inner_partner(way):
        other = lax.rem(shard + (2 if way == 0 else 254), 256)
        return (other // 16, lax.rem(other, 16))

    def outer_partner(i):
        return (lax.rem(c + 4 * i, 16), f)

    barrier = pltpu.get_barrier_semaphore()
    for partner in (inner_partner(0), inner_partner(1), outer_partner(1), outer_partner(2), outer_partner(3)):
        pl.semaphore_signal(barrier, inc=1, device_id=partner, device_id_type=MESH)

    def x_copy(k):
        rows = pl.ds(pl.multiple_of(k * CH, CH), CH)
        return pltpu.make_async_copy(x_hbm.at[rows], x.at[rows], x_sem.at[k])

    weights = [
        pltpu.make_async_copy(src, dst, w_sem.at[i])
        for i, (src, dst) in enumerate(
            (
                (sq_i_hbm, sq_i), (taps_i_hbm, taps_i), (ex_i_hbm, ex_i),
                (sq_o_hbm, sq_o), (taps_o_hbm, taps_o), (ex_o_hbm, ex_o),
            )
        )
    ]
    x_copy(0).start()
    weights[0].start()
    for k in range(1, CHUNKS):
        x_copy(k).start()
    for weight in weights[1:]:
        weight.start()

    def halo(stage, way, k, source, target):
        rows = pl.ds(pl.multiple_of(k * CH, CH), CH)
        return pltpu.make_async_remote_copy(
            src_ref=source.at[rows],
            dst_ref=target.at[rows],
            send_sem=halo_send.at[stage, way, k],
            recv_sem=halo_recv.at[stage, way, k],
            device_id=inner_partner(way),
            device_id_type=MESH,
        )

    def mid_halos(k):
        return halo(0, 0, k, mid, mid_behind), halo(0, 1, k, mid, mid_ahead)

    def dconv_halos(k):
        return halo(1, 0, k, dconv, dconv_behind), halo(1, 1, k, dconv, dconv_ahead)

    def quarter(k, which):
        return pl.ds(pl.multiple_of(k * CH + which * QUARTER, QUARTER), QUARTER)

    def turn(stage, i, k, source, target):
        theirs = lax.rem(mine + i, 4)
        return pltpu.make_async_remote_copy(
            src_ref=source.at[quarter(k, theirs)],
            dst_ref=target.at[quarter(k, mine)],
            send_sem=turn_send.at[stage, i, k],
            recv_sem=turn_recv.at[stage, i, k],
            device_id=outer_partner(i),
            device_id_type=MESH,
        )

    def turns(stage, k):
        source, target = ((xo_send, xo), (g_send, g))[stage]
        return [turn(stage, i, k, source, target) for i in (1, 2, 3)] + [
            pltpu.make_async_copy(source.at[quarter(k, mine)], target.at[quarter(k, mine)], own_sem.at[stage, k])
        ]

    def await_turns(stage, k):
        *remote, own = turns(stage, k)
        for copy in remote:
            copy.wait_recv()
        own.wait()

    def at(k, r, rows=TILE):
        return pl.ds(pl.multiple_of(k * CH + r, TILE), rows)

    def enter(k):
        x_copy(k).wait()

        def first(r):
            n, factor = normed(x[at(k, r), :].astype(F32))
            n_in[at(k, r), :] = n
            f_in[at(k, r), :] = lanes(factor)
            ent[pl.ds(r, TILE), :] = gelu(n).astype(BF16)

        tiles(first)
        narrow[...] = dot(ent[...], sq_i[...])

        def second(r):
            n, factor = normed(narrow[pl.ds(r, TILE), :])
            n_mid[at(k, r), :] = n
            f_mid[at(k, r), :] = lanes(factor)
            mid[at(k, r), :] = gelu(n).astype(BF16)

        tiles(second)

        @pl.when(k < 1)
        def _():
            for copy in mid_halos(k):
                copy.start()

    def prepare(k):
        classes = lax.broadcasted_iota(jnp.int32, (EXTRA, CH), 0)
        columns = (classes == targets[k]).astype(F32).astype(BF16)
        eye = (classes == lax.broadcasted_iota(jnp.int32, (EXTRA, CH), 1)).astype(F32).astype(BF16)
        xo_send[at(k, 0, CH), D:] = dot_t(eye, columns).astype(BF16)

        def first(r):
            sl_in[at(k, r), :] = slope(n_in[at(k, r), :])
            sl_mid[at(k, r), :] = slope(n_mid[at(k, r), :])

        tiles(first)

    def converse(k):
        rows = at(k, 0, CH)
        narrow[...] = dot(mid[rows, :], taps_i[1])
        for copy in mid_halos(k):
            copy.wait_recv()

        @pl.when(k + 1 < CHUNKS)
        def _():
            for copy in mid_halos(k + 1):
                copy.start()

        narrow[...] += dot(mid_behind[rows, :], taps_i[0]) + dot(mid_ahead[rows, :], taps_i[2])

        def first(r):
            n, factor = normed(narrow[pl.ds(r, TILE), :])
            n_conv[at(k, r), :] = n
            f_conv[at(k, r), :] = lanes(factor)
            ent[pl.ds(r, TILE), :BOT] = gelu(n).astype(BF16)

        tiles(first)
        wide[...] = dot(ent[:, :BOT], ex_i[...])

        def second(r):
            xo_send[at(k, r), :D] = (x[at(k, r), :].astype(F32) + wide[pl.ds(r, TILE), :]).astype(BF16)

        tiles(second)
        for copy in turns(0, k):
            copy.start()

    def around(padded):
        padded[pl.ds(0, QUARTER), :] = padded[pl.ds(CH, QUARTER), :]
        padded[pl.ds(QUARTER + CH, QUARTER), :] = padded[pl.ds(QUARTER, QUARTER), :]
        return padded[pl.ds(0, CH), :], padded[pl.ds(QUARTER, CH), :], padded[pl.ds(2 * QUARTER, CH), :]

    def outer(k):
        await_turns(0, k)

        def first(r):
            n, factor = normed(xo[at(k, r), :D].astype(F32))
            o_n_in[pl.ds(r, TILE), :] = n
            o_f_in[pl.ds(r, TILE), :] = lanes(factor)
            ent[pl.ds(r, TILE), :] = gelu(n).astype(BF16)

        tiles(first)
        narrow[...] = dot(ent[...], sq_o[...])

        def second(r):
            n, factor = normed(narrow[pl.ds(r, TILE), :])
            o_n_mid[pl.ds(r, TILE), :] = n
            o_f_mid[pl.ds(r, TILE), :] = lanes(factor)
            o_mid[pl.ds(QUARTER + r, TILE), :] = gelu(n).astype(BF16)

        tiles(second)
        behind, own, ahead = around(o_mid)
        narrow[...] = dot(behind, taps_o[0]) + dot(own, taps_o[1]) + dot(ahead, taps_o[2])

        def third(r):
            n, factor = normed(narrow[pl.ds(r, TILE), :])
            o_n_conv[pl.ds(r, TILE), :] = n
            o_f_conv[pl.ds(r, TILE), :] = lanes(factor)
            ent[pl.ds(r, TILE), :BOT] = gelu(n).astype(BF16)

        tiles(third)
        wide[...] = dot(ent[:, :BOT], ex_o[...])

        def fourth(r):
            final = (xo[at(k, r), :D].astype(F32) + wide[pl.ds(r, TILE), :]).astype(BF16)
            n, factor = normed(final.astype(F32))
            o_grad[pl.ds(r, TILE), :] = n
            narrow[pl.ds(r, TILE), :128] = lanes(factor)
            ent[pl.ds(r, TILE), :] = n.astype(BF16)

        tiles(fourth)
        logits = dot_t(ent[...], dec[...])
        lane = lax.broadcasted_iota(jnp.int32, (CH, EXTRA), 1)
        onehot = xo[at(k, 0, CH), D:].astype(F32)
        exponent = jnp.where(lane < VOCAB, jnp.exp(logits), 0.0)
        totals = jnp.sum(exponent, axis=-1, keepdims=True)
        token_loss = jnp.log(totals) - jnp.sum(logits * onehot, axis=-1, keepdims=True)
        high = token_loss.astype(BF16).astype(F32)
        g_send[at(k, 0, CH), D:] = jnp.where(
            lane == 0, high, jnp.where(lane == 1, token_loss - high, 0.0)
        ).astype(BF16)
        dlogits = (32.0 * (exponent / totals - onehot)).astype(BF16)
        wide[...] = dot(dlogits, dec[...])

        def fifth(r):
            grad = norm_back(o_grad[pl.ds(r, TILE), :], narrow[pl.ds(r, TILE), 0:1], wide[pl.ds(r, TILE), :])
            o_grad[pl.ds(r, TILE), :] = grad
            ent[pl.ds(r, TILE), :] = grad.astype(BF16)

        tiles(fifth)
        narrow[...] = dot_t(ent[...], ex_o[...])

        def sixth(r):
            n = o_n_conv[pl.ds(r, TILE), :]
            upward = slope(n) * narrow[pl.ds(r, TILE), :]
            o_dconv[pl.ds(QUARTER + r, TILE), :] = norm_back(n, o_f_conv[pl.ds(r, TILE), 0:1], upward).astype(BF16)

        tiles(sixth)
        behind, own, ahead = around(o_dconv)
        narrow[...] = dot_t(ahead, taps_o[0]) + dot_t(own, taps_o[1]) + dot_t(behind, taps_o[2])

        def seventh(r):
            n = o_n_mid[pl.ds(r, TILE), :]
            upward = slope(n) * narrow[pl.ds(r, TILE), :]
            ent[pl.ds(r, TILE), :BOT] = norm_back(n, o_f_mid[pl.ds(r, TILE), 0:1], upward).astype(BF16)

        tiles(seventh)
        wide[...] = dot_t(ent[:, :BOT], sq_o[...])

        def eighth(r):
            n = o_n_in[pl.ds(r, TILE), :]
            upward = slope(n) * wide[pl.ds(r, TILE), :]
            back = norm_back(n, o_f_in[pl.ds(r, TILE), 0:1], upward)
            g_send[at(k, r), :D] = (o_grad[pl.ds(r, TILE), :] + back).astype(BF16)

        tiles(eighth)
        for copy in turns(1, k):
            copy.start()

    def turn_back(k):
        await_turns(1, k)
        narrow[...] = dot_t(g[at(k, 0, CH), :D], ex_i[...])

        def first(r):
            n = n_conv[at(k, r), :]
            upward = slope(n) * narrow[pl.ds(r, TILE), :]
            dconv[at(k, r), :] = norm_back(n, f_conv[at(k, r), 0:1], upward).astype(BF16)

        tiles(first)
        for copy in dconv_halos(k):
            copy.start()

    def leave(k):
        loss_out[k] = dot_t(jnp.ones((8, EXTRA), BF16), g[at(k, 0, CH), D:])[0:1]
        rows = at(k, 0, CH)
        narrow[...] = dot_t(dconv[rows, :], taps_i[1])
        for copy in dconv_halos(k):
            copy.wait_recv()
        narrow[...] += dot_t(dconv_ahead[rows, :], taps_i[0]) + dot_t(dconv_behind[rows, :], taps_i[2])

        def first(r):
            upward = sl_mid[at(k, r), :] * narrow[pl.ds(r, TILE), :]
            ent[pl.ds(r, TILE), :BOT] = norm_back(n_mid[at(k, r), :], f_mid[at(k, r), 0:1], upward).astype(BF16)

        tiles(first)
        wide[...] = dot_t(ent[:, :BOT], sq_i[...])

        def second(r):
            upward = sl_in[at(k, r), :] * wide[pl.ds(r, TILE), :]
            back = norm_back(n_in[at(k, r), :], f_in[at(k, r), 0:1], upward)
            outs[at(k, r), :] = (g[at(k, r), :D].astype(F32) + back).astype(BF16)

        tiles(second)

    def loop(count, body):
        def step(k, carry):
            body(k)
            return carry

        lax.fori_loop(0, count, step, 0)

    dec[...] = jnp.zeros_like(dec)
    dec[pl.ds(0, VOCAB), :] = decoder[...]
    pl.semaphore_wait(barrier, 5)
    weights[0].wait()
    loop(CHUNKS, enter)
    loop(CHUNKS, prepare)
    for weight in weights[1:]:
        weight.wait()

    def middle(step):
        s = step - 1

        @pl.when(s + 1 < CHUNKS)
        def _():
            converse(s + 1)

        @pl.when(jnp.logical_and(s >= 0, s < CHUNKS))
        def _():
            outer(s)

        @pl.when(s >= 1)
        def _():
            turn_back(s - 1)

    loop(CHUNKS + 2, middle)
    loop(CHUNKS, leave)

    def finish(k):
        for copy in mid_halos(k) + dconv_halos(k):
            copy.wait_send()
        for stage in (0, 1):
            for copy in turns(stage, k)[:3]:
                copy.wait_send()

    loop(CHUNKS, finish)


def on_device(activations, targets, sq_i, taps_i, ex_i, sq_o, taps_o, ex_o, decoder):
    anywhere = pl.BlockSpec(memory_space=pltpu.HBM)
    vmem = pl.BlockSpec(memory_space=pltpu.VMEM)
    targets = targets.reshape(CHUNKS, 1, CH)
    v = pltpu.VMEM
    dma = pltpu.SemaphoreType.DMA
    out, loss = pl.pallas_call(
        kernel,
        out_shape=(
            pltpu.VMEM((ROWS, D), BF16),
            pltpu.VMEM((CHUNKS, 1, CH), F32),
        ),
        in_specs=[anywhere, vmem, vmem] + [anywhere] * 6,
        out_specs=(vmem, vmem),
        scratch_shapes=[
            v((ROWS, D), BF16),
            v((D, BOT), BF16), v((3, BOT, BOT), BF16), v((BOT, D), BF16),
            v((D, BOT), BF16), v((3, BOT, BOT), BF16), v((BOT, D), BF16),
            v((ROWS, D), F32), v((ROWS, 128), F32),
            v((ROWS, BOT), F32), v((ROWS, 128), F32),
            v((ROWS, BOT), F32), v((ROWS, 128), F32),
            v((ROWS, D), F32), v((ROWS, BOT), F32),
            v((ROWS, BOT), BF16), v((ROWS, BOT), BF16), v((ROWS, BOT), BF16),
            v((ROWS, BOT), BF16), v((ROWS, BOT), BF16), v((ROWS, BOT), BF16),
            v((ROWS, WIDE), BF16), v((ROWS, WIDE), BF16), v((ROWS, WIDE), BF16), v((ROWS, WIDE), BF16),
            v((CH, D), BF16), v((CH, D), F32), v((CH, BOT), F32),
            v((CH, D), F32), v((CH, 128), F32), v((CH, BOT), F32), v((CH, 128), F32),
            v((CH, BOT), F32), v((CH, 128), F32), v((CH, D), F32),
            v((CH + 2 * QUARTER, BOT), BF16), v((CH + 2 * QUARTER, BOT), BF16), v((EXTRA, D), BF16),
            dma((6,)), dma((CHUNKS,)), dma((2, CHUNKS)),
            dma((2, 2, CHUNKS)), dma((2, 2, CHUNKS)), dma((2, 4, CHUNKS)), dma((2, 4, CHUNKS)),
        ],
        compiler_params=pltpu.CompilerParams(
            collective_id=0, has_side_effects=True, vmem_limit_bytes=62 * 1024 * 1024
        ),
    )(activations, targets, decoder, sq_i, taps_i, ex_i, sq_o, taps_o, ex_o)
    return out, loss.reshape(ROWS)


def solution(mesh):
    rows = P(("coarse", "fine"))
    return jax.shard_map(
        on_device,
        mesh=mesh,
        in_specs=(P(("coarse", "fine"), None), rows, P(), P(), P(), P(), P(), P(), P()),
        out_specs=(P(("coarse", "fine"), None), rows),
        check_vma=False,
    )
```

```python
import functools
import math

import jax
import jax.numpy as jnp
from jax import lax
from jax.experimental import pallas as pl
from jax.experimental.pallas import tpu as pltpu
from jax.sharding import PartitionSpec as P

MESH = pl.DeviceIdType.MESH
F32, BF16 = jnp.float32, jnp.bfloat16
EPS = 1e-05
ROWS, D, BOT, VOCAB = 512, 1280, 640, 5
CHUNKS = 4
CH = ROWS // CHUNKS
QUARTER = CH // 4
EXTRA = 128
AHEAD = 4
TILE = 16


def normed(values):
    centred = values - jnp.mean(values, axis=-1, keepdims=True)
    factor = lax.rsqrt(jnp.mean(centred * centred, axis=-1, keepdims=True) + EPS)
    return centred * factor, factor


def norm_back(normal, factor, upward):
    first = upward - jnp.mean(upward, axis=-1, keepdims=True)
    return (first - normal * jnp.mean(upward * normal, axis=-1, keepdims=True)) * factor


def gelu(s):
    return 0.5 * s * (1.0 + lax.erf(s * (1.0 / math.sqrt(2.0))))


def slope(s):
    return 0.5 * (1.0 + lax.erf(s * (1.0 / math.sqrt(2.0)))) + s * jnp.exp(-0.5 * s * s) * (
        1.0 / math.sqrt(2.0 * math.pi)
    )


def dot(a, b):
    return jnp.dot(a, b, preferred_element_type=F32)


def dot_t(a, b):
    return lax.dot_general(a, b, (((1,), (1,)), ((), ())), preferred_element_type=F32)


def tiles(body, unroll=CH // TILE):
    def step(i, carry):
        body(pl.multiple_of(i * TILE, TILE))
        return carry

    lax.fori_loop(0, CH // TILE, step, 0, unroll=unroll)


def lanes(column):
    return jnp.broadcast_to(column, (column.shape[0], 128))


def kernel(
    x_hbm, targets, decoder, sq_i_hbm, taps_i_hbm, ex_i_hbm, sq_o_hbm, taps_o_hbm, ex_o_hbm,
    outs, loss_out,
    x, sq_i, taps_i, ex_i, sq_o, taps_o, ex_o,
    n_in, f_in, n_mid, f_mid, n_conv, f_conv, sl_in, sl_mid,
    mid, mid_behind, mid_ahead, dconv, dconv_behind, dconv_ahead,
    xo, g, outs_send, hot_send, hot, loss_send, loss_back,
    ent, wide, narrow,
    o_n_in, o_f_in, o_n_mid, o_f_mid, o_n_conv, o_f_conv, o_grad, o_mid, o_dconv, dec,
    w_sem, own_sem, halo_send, halo_recv, turn_send, turn_recv,
):
    c, f = lax.axis_index("coarse"), lax.axis_index("fine")
    shard = c * 16 + f
    mine = c // 4

    along = lax.rem(c, 4) * 16 + f

    def inner_partner(way):
        other = lax.rem(along + (2 if way == 0 else 62), 64)
        return (mine * 4 + other // 16, lax.rem(other, 16))

    shifts = ((along + 2) // 64, 3 * (1 - (along + 62) // 64))

    def outer_partner(i):
        return (lax.rem(c + 4 * i, 16), f)

    barrier = pltpu.get_barrier_semaphore()
    for partner in (inner_partner(0), inner_partner(1), outer_partner(1), outer_partner(2), outer_partner(3)):
        pl.semaphore_signal(barrier, inc=1, device_id=partner, device_id_type=MESH)

    weights = [
        pltpu.make_async_copy(src, dst, w_sem.at[i])
        for i, (src, dst) in enumerate(
            (
                (sq_i_hbm, sq_i), (taps_i_hbm, taps_i), (ex_i_hbm, ex_i),
                (sq_o_hbm, sq_o), (taps_o_hbm, taps_o), (ex_o_hbm, ex_o),
            )
        )
    ]
    for weight in weights:
        weight.start()

    def copy_rows(stage, way, k, source, source_rows, target, target_rows):
        return pltpu.make_async_remote_copy(
            src_ref=source.at[source_rows],
            dst_ref=target.at[target_rows],
            send_sem=halo_send.at[stage, way, k],
            recv_sem=halo_recv.at[stage, way, k],
            device_id=inner_partner(way),
            device_id_type=MESH,
        )

    def halo(stage, way, k, source, target):
        rows = pl.ds(pl.multiple_of(k * CH, CH), CH)
        return copy_rows(stage, way, k, source, rows, target, rows)

    def send_halos(stage, k, source, targets_pair):
        for way in (0, 1):
            for block in range(4):
                there = lax.rem(block + shifts[way], 4)
                copy_rows(
                    stage, way, k, source, quarter(k, block), targets_pair[way], quarter(k, there)
                ).start()

    def mid_halos(k):
        return halo(0, 0, k, mid, mid_behind), halo(0, 1, k, mid, mid_ahead)

    def dconv_halos(k):
        return halo(1, 0, k, dconv, dconv_behind), halo(1, 1, k, dconv, dconv_ahead)

    def quarter(k, which):
        return pl.ds(pl.multiple_of(k * CH + which * QUARTER, QUARTER), QUARTER)

    def turn(stage, i, k, source, target):
        theirs = lax.rem(mine + i, 4)
        return pltpu.make_async_remote_copy(
            src_ref=source.at[quarter(k, theirs)],
            dst_ref=target.at[quarter(k, mine)],
            send_sem=turn_send.at[stage, i, k],
            recv_sem=turn_recv.at[stage, i, k],
            device_id=outer_partner(i),
            device_id_type=MESH,
        )

    def turns(stage, k):
        source, target = ((x_hbm, x), (outs_send, outs), (hot_send, hot), (loss_send, loss_back))[stage]
        return [turn(stage, i, k, source, target) for i in (1, 2, 3)] + [
            pltpu.make_async_copy(source.at[quarter(k, mine)], target.at[quarter(k, mine)], own_sem.at[stage, k])
        ]

    def await_turns(stage, k):
        *remote, own = turns(stage, k)
        for copy in remote:
            copy.wait_recv()
        own.wait()

    def at(k, r, rows=TILE):
        return pl.ds(pl.multiple_of(k * CH + r, TILE), rows)

    def enter(k):
        await_turns(0, k)

        def first(r):
            n, factor = normed(x[at(k, r), :].astype(F32))
            n_in[at(k, r), :] = n
            f_in[at(k, r), :] = lanes(factor)
            ent[pl.ds(r, TILE), :] = gelu(n).astype(BF16)

        tiles(first)
        narrow[...] = dot(ent[...], sq_i[...])

        def second(r):
            n, factor = normed(narrow[pl.ds(r, TILE), :])
            n_mid[at(k, r), :] = n
            f_mid[at(k, r), :] = lanes(factor)
            mid[at(k, r), :] = gelu(n).astype(BF16)

        tiles(second)

        @pl.when(k < AHEAD)
        def _():
            send_halos(0, k, mid, (mid_behind, mid_ahead))

    def prepare(k):
        classes = lax.broadcasted_iota(jnp.int32, (EXTRA, CH), 0)
        columns = (classes == targets[k]).astype(F32).astype(BF16)
        eye = (classes == lax.broadcasted_iota(jnp.int32, (EXTRA, CH), 1)).astype(F32).astype(BF16)
        hot_send[at(k, 0, CH), :] = dot_t(eye, columns).astype(BF16)
        for copy in turns(2, k):
            copy.start()

        def first(r):
            sl_in[at(k, r), :] = slope(n_in[at(k, r), :])
            sl_mid[at(k, r), :] = slope(n_mid[at(k, r), :])

        tiles(first)

    def converse(k):
        rows = at(k, 0, CH)
        narrow[...] = dot(mid[rows, :], taps_i[1])
        for copy in mid_halos(k):
            copy.wait_recv()

        @pl.when(k + AHEAD < CHUNKS)
        def _():
            send_halos(0, k + AHEAD, mid, (mid_behind, mid_ahead))

        narrow[...] += dot(mid_behind[rows, :], taps_i[0]) + dot(mid_ahead[rows, :], taps_i[2])

        def first(r):
            n, factor = normed(narrow[pl.ds(r, TILE), :])
            n_conv[pl.ds(r, TILE), :] = n
            f_conv[pl.ds(r, TILE), :] = lanes(factor)
            ent[pl.ds(r, TILE), :BOT] = gelu(n).astype(BF16)

        tiles(first)
        wide[...] = dot(ent[:, :BOT], ex_i[...])

        def second(r):
            xo[pl.ds(r, TILE), :] = (x[at(k, r), :].astype(F32) + wide[pl.ds(r, TILE), :]).astype(BF16)

        tiles(second)

    def around(padded):
        padded[pl.ds(0, QUARTER), :] = padded[pl.ds(CH, QUARTER), :]
        padded[pl.ds(QUARTER + CH, QUARTER), :] = padded[pl.ds(QUARTER, QUARTER), :]
        return padded[pl.ds(0, CH), :], padded[pl.ds(QUARTER, CH), :], padded[pl.ds(2 * QUARTER, CH), :]

    def outer(k):
        def first(r):
            n, factor = normed(xo[pl.ds(r, TILE), :].astype(F32))
            o_n_in[pl.ds(r, TILE), :] = n
            o_f_in[pl.ds(r, TILE), :] = lanes(factor)
            ent[pl.ds(r, TILE), :] = gelu(n).astype(BF16)

        tiles(first)
        narrow[...] = dot(ent[...], sq_o[...])

        def second(r):
            n, factor = normed(narrow[pl.ds(r, TILE), :])
            o_n_mid[pl.ds(r, TILE), :] = n
            o_f_mid[pl.ds(r, TILE), :] = lanes(factor)
            o_mid[pl.ds(QUARTER + r, TILE), :] = gelu(n).astype(BF16)

        tiles(second)
        behind, own, ahead = around(o_mid)
        narrow[...] = dot(behind, taps_o[0]) + dot(own, taps_o[1]) + dot(ahead, taps_o[2])

        def third(r):
            n, factor = normed(narrow[pl.ds(r, TILE), :])
            o_n_conv[pl.ds(r, TILE), :] = n
            o_f_conv[pl.ds(r, TILE), :] = lanes(factor)
            ent[pl.ds(r, TILE), :BOT] = gelu(n).astype(BF16)

        tiles(third)
        wide[...] = dot(ent[:, :BOT], ex_o[...])

        def fourth(r):
            final = (xo[pl.ds(r, TILE), :].astype(F32) + wide[pl.ds(r, TILE), :]).astype(BF16)
            n, factor = normed(final.astype(F32))
            o_grad[pl.ds(r, TILE), :] = n
            narrow[pl.ds(r, TILE), :128] = lanes(factor)
            ent[pl.ds(r, TILE), :] = n.astype(BF16)

        tiles(fourth)
        logits = dot_t(ent[...], dec[...])
        await_turns(2, k)
        lane = lax.broadcasted_iota(jnp.int32, (CH, EXTRA), 1)
        onehot = hot[at(k, 0, CH), :].astype(F32)
        exponent = jnp.where(lane < VOCAB, jnp.exp(logits), 0.0)
        totals = jnp.sum(exponent, axis=-1, keepdims=True)
        token_loss = jnp.log(totals) - jnp.sum(logits * onehot, axis=-1, keepdims=True)
        high = token_loss.astype(BF16).astype(F32)
        loss_send[at(k, 0, CH), :] = jnp.where(
            lane == 0, high, jnp.where(lane == 1, token_loss - high, 0.0)
        ).astype(BF16)
        for copy in turns(3, k):
            copy.start()
        dlogits = (32.0 * (exponent / totals - onehot)).astype(BF16)
        wide[...] = dot(dlogits, dec[...])

        def fifth(r):
            grad = norm_back(o_grad[pl.ds(r, TILE), :], narrow[pl.ds(r, TILE), 0:1], wide[pl.ds(r, TILE), :])
            o_grad[pl.ds(r, TILE), :] = grad
            ent[pl.ds(r, TILE), :] = grad.astype(BF16)

        tiles(fifth)
        narrow[...] = dot_t(ent[...], ex_o[...])

        def sixth(r):
            n = o_n_conv[pl.ds(r, TILE), :]
            upward = slope(n) * narrow[pl.ds(r, TILE), :]
            o_dconv[pl.ds(QUARTER + r, TILE), :] = norm_back(n, o_f_conv[pl.ds(r, TILE), 0:1], upward).astype(BF16)

        tiles(sixth)
        behind, own, ahead = around(o_dconv)
        narrow[...] = dot_t(ahead, taps_o[0]) + dot_t(own, taps_o[1]) + dot_t(behind, taps_o[2])

        def seventh(r):
            n = o_n_mid[pl.ds(r, TILE), :]
            upward = slope(n) * narrow[pl.ds(r, TILE), :]
            ent[pl.ds(r, TILE), :BOT] = norm_back(n, o_f_mid[pl.ds(r, TILE), 0:1], upward).astype(BF16)

        tiles(seventh)
        wide[...] = dot_t(ent[:, :BOT], sq_o[...])

        def eighth(r):
            n = o_n_in[pl.ds(r, TILE), :]
            upward = slope(n) * wide[pl.ds(r, TILE), :]
            back = norm_back(n, o_f_in[pl.ds(r, TILE), 0:1], upward)
            total = o_grad[pl.ds(r, TILE), :] + back
            g[at(k, r), :] = total
            ent[pl.ds(r, TILE), :] = total.astype(BF16)

        tiles(eighth)

    def turn_back(k):
        narrow[...] = dot_t(ent[...], ex_i[...])

        def first(r):
            n = n_conv[pl.ds(r, TILE), :]
            upward = slope(n) * narrow[pl.ds(r, TILE), :]
            dconv[at(k, r), :] = norm_back(n, f_conv[pl.ds(r, TILE), 0:1], upward).astype(BF16)

        tiles(first)
        send_halos(1, k, dconv, (dconv_behind, dconv_ahead))

    def leave(k):
        rows = at(k, 0, CH)
        narrow[...] = dot_t(dconv[rows, :], taps_i[1])
        for copy in dconv_halos(k):
            copy.wait_recv()
        narrow[...] += dot_t(dconv_ahead[rows, :], taps_i[0]) + dot_t(dconv_behind[rows, :], taps_i[2])

        def first(r):
            upward = sl_mid[at(k, r), :] * narrow[pl.ds(r, TILE), :]
            ent[pl.ds(r, TILE), :BOT] = norm_back(n_mid[at(k, r), :], f_mid[at(k, r), 0:1], upward).astype(BF16)

        tiles(first)
        wide[...] = dot_t(ent[:, :BOT], sq_i[...])

        def second(r):
            upward = sl_in[at(k, r), :] * wide[pl.ds(r, TILE), :]
            back = norm_back(n_in[at(k, r), :], f_in[at(k, r), 0:1], upward)
            outs_send[at(k, r), :] = (g[at(k, r), :] + back).astype(BF16)

        tiles(second)
        for copy in turns(1, k):
            copy.start()

    def loop(count, body):
        def step(k, carry):
            body(k)
            return carry

        lax.fori_loop(0, count, step, 0)

    dec[...] = jnp.zeros_like(dec)
    dec[pl.ds(0, VOCAB), :] = decoder[...]
    pl.semaphore_wait(barrier, 5)

    def fetch(k):
        for copy in turns(0, k):
            copy.start()

    loop(CHUNKS, fetch)
    weights[0].wait()
    loop(CHUNKS, enter)
    loop(CHUNKS, prepare)
    for weight in weights[1:]:
        weight.wait()

    def middle(k):
        converse(k)
        outer(k)
        turn_back(k)

    loop(CHUNKS, middle)
    loop(CHUNKS, leave)

    def finish(k):
        for copy in mid_halos(k) + dconv_halos(k):
            copy.wait_send()
        await_turns(3, k)
        loss_out[k] = dot_t(jnp.ones((8, EXTRA), BF16), loss_back[at(k, 0, CH), :])[0:1]
        await_turns(1, k)
        for stage in range(4):
            for copy in turns(stage, k)[:3]:
                copy.wait_send()

    loop(CHUNKS, finish)


def on_device(activations, targets, sq_i, taps_i, ex_i, sq_o, taps_o, ex_o, decoder):
    anywhere = pl.BlockSpec(memory_space=pltpu.HBM)
    vmem = pl.BlockSpec(memory_space=pltpu.VMEM)
    targets = targets.reshape(CHUNKS, 1, CH)
    v = pltpu.VMEM
    dma = pltpu.SemaphoreType.DMA
    out, loss = pl.pallas_call(
        kernel,
        out_shape=(
            pltpu.VMEM((ROWS, D), BF16),
            pltpu.VMEM((CHUNKS, 1, CH), F32),
        ),
        in_specs=[anywhere, vmem, vmem] + [anywhere] * 6,
        out_specs=(vmem, vmem),
        scratch_shapes=[
            v((ROWS, D), BF16),
            v((D, BOT), BF16), v((3, BOT, BOT), BF16), v((BOT, D), BF16),
            v((D, BOT), BF16), v((3, BOT, BOT), BF16), v((BOT, D), BF16),
            v((ROWS, D), F32), v((ROWS, 128), F32),
            v((ROWS, BOT), F32), v((ROWS, 128), F32),
            v((ROWS, BOT), F32), v((ROWS, 128), F32),
            v((ROWS, D), F32), v((ROWS, BOT), F32),
            v((ROWS, BOT), BF16), v((ROWS, BOT), BF16), v((ROWS, BOT), BF16),
            v((ROWS, BOT), BF16), v((ROWS, BOT), BF16), v((ROWS, BOT), BF16),
            v((CH, D), BF16), v((ROWS, D), F32), v((ROWS, D), BF16),
            v((ROWS, EXTRA), BF16), v((ROWS, EXTRA), BF16), v((ROWS, EXTRA), BF16), v((ROWS, EXTRA), BF16),
            v((CH, D), BF16), v((CH, D), F32), v((CH, BOT), F32),
            v((CH, D), F32), v((CH, 128), F32), v((CH, BOT), F32), v((CH, 128), F32),
            v((CH, BOT), F32), v((CH, 128), F32), v((CH, D), F32),
            v((CH + 2 * QUARTER, BOT), BF16), v((CH + 2 * QUARTER, BOT), BF16), v((EXTRA, D), BF16),
            dma((6,)), dma((4, CHUNKS)),
            dma((2, 2, CHUNKS)), dma((2, 2, CHUNKS)), dma((4, 4, CHUNKS)), dma((4, 4, CHUNKS)),
        ],
        compiler_params=pltpu.CompilerParams(
            collective_id=0, has_side_effects=True, vmem_limit_bytes=62 * 1024 * 1024
        ),
    )(activations, targets, decoder, sq_i, taps_i, ex_i, sq_o, taps_o, ex_o)
    return out, loss.reshape(ROWS)


def solution(mesh):
    rows = P(("coarse", "fine"))
    return jax.shard_map(
        on_device,
        mesh=mesh,
        in_specs=(P(("coarse", "fine"), None), rows, P(), P(), P(), P(), P(), P(), P()),
        out_specs=(P(("coarse", "fine"), None), rows),
        check_vma=False,
    )
```

```python
import functools
import math

import jax
import jax.numpy as jnp
from jax import lax
from jax.experimental import pallas as pl
from jax.experimental.pallas import tpu as pltpu
from jax.sharding import PartitionSpec as P

MESH = pl.DeviceIdType.MESH
F32, BF16 = jnp.float32, jnp.bfloat16
EPS = 1e-05
ROWS, D, BOT, VOCAB = 512, 1280, 640, 5
CHUNKS = 4
CH = ROWS // CHUNKS
QUARTER = CH // 4
EXTRA = 128
AHEAD = 3
TILE = 16


def normed(values):
    centred = values - jnp.mean(values, axis=-1, keepdims=True)
    factor = lax.rsqrt(jnp.mean(centred * centred, axis=-1, keepdims=True) + EPS)
    return centred * factor, factor


def norm_back(normal, factor, upward):
    first = upward - jnp.mean(upward, axis=-1, keepdims=True)
    return (first - normal * jnp.mean(upward * normal, axis=-1, keepdims=True)) * factor


def gelu(s):
    return 0.5 * s * (1.0 + lax.erf(s * (1.0 / math.sqrt(2.0))))


def slope(s):
    return 0.5 * (1.0 + lax.erf(s * (1.0 / math.sqrt(2.0)))) + s * jnp.exp(-0.5 * s * s) * (
        1.0 / math.sqrt(2.0 * math.pi)
    )


def dot(a, b):
    return jnp.dot(a, b, preferred_element_type=F32)


def dot_t(a, b):
    return lax.dot_general(a, b, (((1,), (1,)), ((), ())), preferred_element_type=F32)


def tiles(body, unroll=CH // TILE):
    def step(i, carry):
        body(pl.multiple_of(i * TILE, TILE))
        return carry

    lax.fori_loop(0, CH // TILE, step, 0, unroll=unroll)


def lanes(column):
    return jnp.broadcast_to(column, (column.shape[0], 128))


def kernel(
    x_hbm, targets, decoder, sq_i_hbm, taps_i_hbm, ex_i_hbm, sq_o_hbm, taps_o_hbm, ex_o_hbm,
    outs, loss_out,
    x, sq_i, taps_i, ex_i, sq_o, taps_o, ex_o,
    n_in, f_in, n_mid, f_mid, n_conv, f_conv, sl_in, sl_mid,
    mid, mid_behind, mid_ahead, dconv, dconv_behind, dconv_ahead,
    xo, g, outs_send, hot_send, hot, loss_send, loss_back,
    ent, wide, narrow,
    o_n_in, o_f_in, o_n_mid, o_f_mid, o_n_conv, o_f_conv, o_grad, o_mid, o_dconv, dec,
    w_sem, own_sem, halo_send, halo_recv, turn_send, turn_recv,
):
    c, f = lax.axis_index("coarse"), lax.axis_index("fine")
    shard = c * 16 + f
    mine = c // 4

    along = lax.rem(c, 4) * 16 + f

    def inner_partner(way):
        other = lax.rem(along + (2 if way == 0 else 62), 64)
        return (mine * 4 + other // 16, lax.rem(other, 16))

    shifts = ((along + 2) // 64, 3 * (1 - (along + 62) // 64))

    def outer_partner(i):
        return (lax.rem(c + 4 * i, 16), f)

    barrier = pltpu.get_barrier_semaphore()
    for partner in (inner_partner(0), inner_partner(1), outer_partner(1), outer_partner(2), outer_partner(3)):
        pl.semaphore_signal(barrier, inc=1, device_id=partner, device_id_type=MESH)

    weights = [
        pltpu.make_async_copy(src, dst, w_sem.at[i])
        for i, (src, dst) in enumerate(
            (
                (sq_i_hbm, sq_i), (taps_i_hbm, taps_i), (ex_i_hbm, ex_i),
                (sq_o_hbm, sq_o), (taps_o_hbm, taps_o), (ex_o_hbm, ex_o),
            )
        )
    ]
    for weight in weights:
        weight.start()

    def copy_rows(stage, way, k, source, source_rows, target, target_rows):
        return pltpu.make_async_remote_copy(
            src_ref=source.at[source_rows],
            dst_ref=target.at[target_rows],
            send_sem=halo_send.at[stage, way, k],
            recv_sem=halo_recv.at[stage, way, k],
            device_id=inner_partner(way),
            device_id_type=MESH,
        )

    def halo(stage, way, k, source, target):
        rows = pl.ds(pl.multiple_of(k * CH, CH), CH)
        return copy_rows(stage, way, k, source, rows, target, rows)

    def send_halos(stage, k, source, targets_pair):
        for way in (0, 1):
            for block in range(4):
                there = lax.rem(block + shifts[way], 4)
                copy_rows(
                    stage, way, k, source, quarter(k, block), targets_pair[way], quarter(k, there)
                ).start()

    def mid_halos(k):
        return halo(0, 0, k, mid, mid_behind), halo(0, 1, k, mid, mid_ahead)

    def dconv_halos(k):
        return halo(1, 0, k, dconv, dconv_behind), halo(1, 1, k, dconv, dconv_ahead)

    def quarter(k, which):
        return pl.ds(pl.multiple_of(k * CH + which * QUARTER, QUARTER), QUARTER)

    def turn(stage, i, k, source, target):
        theirs = lax.rem(mine + i, 4)
        return pltpu.make_async_remote_copy(
            src_ref=source.at[quarter(k, theirs)],
            dst_ref=target.at[quarter(k, mine)],
            send_sem=turn_send.at[stage, i, k],
            recv_sem=turn_recv.at[stage, i, k],
            device_id=outer_partner(i),
            device_id_type=MESH,
        )

    def turns(stage, k):
        source, target = ((x_hbm, x), (outs_send, outs), (hot_send, hot), (loss_send, loss_back))[stage]
        return [turn(stage, i, k, source, target) for i in (1, 2, 3)] + [
            pltpu.make_async_copy(source.at[quarter(k, mine)], target.at[quarter(k, mine)], own_sem.at[stage, k])
        ]

    def await_turns(stage, k):
        *remote, own = turns(stage, k)
        for copy in remote:
            copy.wait_recv()
        own.wait()

    def at(k, r, rows=TILE):
        return pl.ds(pl.multiple_of(k * CH + r, TILE), rows)

    def enter(k):
        await_turns(0, k)

        def first(r):
            n, factor = normed(x[at(k, r), :].astype(F32))
            n_in[at(k, r), :] = n
            f_in[at(k, r), :] = lanes(factor)
            ent[pl.ds(r, TILE), :] = gelu(n).astype(BF16)

        tiles(first)
        narrow[...] = dot(ent[...], sq_i[...])

        def second(r):
            n, factor = normed(narrow[pl.ds(r, TILE), :])
            n_mid[at(k, r), :] = n
            f_mid[at(k, r), :] = lanes(factor)
            mid[at(k, r), :] = gelu(n).astype(BF16)

        tiles(second)

        @pl.when(k < AHEAD)
        def _():
            send_halos(0, k, mid, (mid_behind, mid_ahead))

    def prepare(k):
        classes = lax.broadcasted_iota(jnp.int32, (EXTRA, CH), 0)
        columns = (classes == targets[k]).astype(F32).astype(BF16)
        eye = (classes == lax.broadcasted_iota(jnp.int32, (EXTRA, CH), 1)).astype(F32).astype(BF16)
        hot_send[at(k, 0, CH), :] = dot_t(eye, columns).astype(BF16)
        for copy in turns(2, k):
            copy.start()

        def first(r):
            sl_in[at(k, r), :] = slope(n_in[at(k, r), :])
            sl_mid[at(k, r), :] = slope(n_mid[at(k, r), :])

        tiles(first)

    def converse(k):
        rows = at(k, 0, CH)
        narrow[...] = dot(mid[rows, :], taps_i[1])
        for copy in mid_halos(k):
            copy.wait_recv()

        @pl.when(k + AHEAD < CHUNKS)
        def _():
            send_halos(0, k + AHEAD, mid, (mid_behind, mid_ahead))

        narrow[...] += dot(mid_behind[rows, :], taps_i[0]) + dot(mid_ahead[rows, :], taps_i[2])

        def first(r):
            n, factor = normed(narrow[pl.ds(r, TILE), :])
            n_conv[pl.ds(r, TILE), :] = n
            f_conv[pl.ds(r, TILE), :] = lanes(factor)
            ent[pl.ds(r, TILE), :BOT] = gelu(n).astype(BF16)

        tiles(first)
        wide[...] = dot(ent[:, :BOT], ex_i[...])

        def second(r):
            xo[pl.ds(r, TILE), :] = (x[at(k, r), :].astype(F32) + wide[pl.ds(r, TILE), :]).astype(BF16)

        tiles(second)

    def around(padded):
        padded[pl.ds(0, QUARTER), :] = padded[pl.ds(CH, QUARTER), :]
        padded[pl.ds(QUARTER + CH, QUARTER), :] = padded[pl.ds(QUARTER, QUARTER), :]
        return padded[pl.ds(0, CH), :], padded[pl.ds(QUARTER, CH), :], padded[pl.ds(2 * QUARTER, CH), :]

    def outer(k):
        def first(r):
            n, factor = normed(xo[pl.ds(r, TILE), :].astype(F32))
            o_n_in[pl.ds(r, TILE), :] = n
            o_f_in[pl.ds(r, TILE), :] = lanes(factor)
            ent[pl.ds(r, TILE), :] = gelu(n).astype(BF16)

        tiles(first)
        narrow[...] = dot(ent[...], sq_o[...])

        def second(r):
            n, factor = normed(narrow[pl.ds(r, TILE), :])
            o_n_mid[pl.ds(r, TILE), :] = n
            o_f_mid[pl.ds(r, TILE), :] = lanes(factor)
            o_mid[pl.ds(QUARTER + r, TILE), :] = gelu(n).astype(BF16)

        tiles(second)
        behind, own, ahead = around(o_mid)
        narrow[...] = dot(behind, taps_o[0]) + dot(own, taps_o[1]) + dot(ahead, taps_o[2])

        def third(r):
            n, factor = normed(narrow[pl.ds(r, TILE), :])
            o_n_conv[pl.ds(r, TILE), :] = n
            o_f_conv[pl.ds(r, TILE), :] = lanes(factor)
            ent[pl.ds(r, TILE), :BOT] = gelu(n).astype(BF16)

        tiles(third)
        wide[...] = dot(ent[:, :BOT], ex_o[...])

        def fourth(r):
            final = (xo[pl.ds(r, TILE), :].astype(F32) + wide[pl.ds(r, TILE), :]).astype(BF16)
            n, factor = normed(final.astype(F32))
            o_grad[pl.ds(r, TILE), :] = n
            narrow[pl.ds(r, TILE), :128] = lanes(factor)
            ent[pl.ds(r, TILE), :] = n.astype(BF16)

        tiles(fourth)
        logits = dot_t(ent[...], dec[...])
        await_turns(2, k)
        lane = lax.broadcasted_iota(jnp.int32, (CH, EXTRA), 1)
        onehot = hot[at(k, 0, CH), :].astype(F32)
        exponent = jnp.where(lane < VOCAB, jnp.exp(logits), 0.0)
        totals = jnp.sum(exponent, axis=-1, keepdims=True)
        token_loss = jnp.log(totals) - jnp.sum(logits * onehot, axis=-1, keepdims=True)
        high = token_loss.astype(BF16).astype(F32)
        loss_send[at(k, 0, CH), :] = jnp.where(
            lane == 0, high, jnp.where(lane == 1, token_loss - high, 0.0)
        ).astype(BF16)
        for copy in turns(3, k):
            copy.start()
        dlogits = (32.0 * (exponent / totals - onehot)).astype(BF16)
        wide[...] = dot(dlogits, dec[...])

        def fifth(r):
            grad = norm_back(o_grad[pl.ds(r, TILE), :], narrow[pl.ds(r, TILE), 0:1], wide[pl.ds(r, TILE), :])
            o_grad[pl.ds(r, TILE), :] = grad
            ent[pl.ds(r, TILE), :] = grad.astype(BF16)

        tiles(fifth)
        narrow[...] = dot_t(ent[...], ex_o[...])

        def sixth(r):
            n = o_n_conv[pl.ds(r, TILE), :]
            upward = slope(n) * narrow[pl.ds(r, TILE), :]
            o_dconv[pl.ds(QUARTER + r, TILE), :] = norm_back(n, o_f_conv[pl.ds(r, TILE), 0:1], upward).astype(BF16)

        tiles(sixth)
        behind, own, ahead = around(o_dconv)
        narrow[...] = dot_t(ahead, taps_o[0]) + dot_t(own, taps_o[1]) + dot_t(behind, taps_o[2])

        def seventh(r):
            n = o_n_mid[pl.ds(r, TILE), :]
            upward = slope(n) * narrow[pl.ds(r, TILE), :]
            ent[pl.ds(r, TILE), :BOT] = norm_back(n, o_f_mid[pl.ds(r, TILE), 0:1], upward).astype(BF16)

        tiles(seventh)
        wide[...] = dot_t(ent[:, :BOT], sq_o[...])

        def eighth(r):
            n = o_n_in[pl.ds(r, TILE), :]
            upward = slope(n) * wide[pl.ds(r, TILE), :]
            back = norm_back(n, o_f_in[pl.ds(r, TILE), 0:1], upward)
            total = o_grad[pl.ds(r, TILE), :] + back
            g[at(k, r), :] = total
            ent[pl.ds(r, TILE), :] = total.astype(BF16)

        tiles(eighth)

    def turn_back(k):
        narrow[...] = dot_t(ent[...], ex_i[...])

        def first(r):
            n = n_conv[pl.ds(r, TILE), :]
            upward = slope(n) * narrow[pl.ds(r, TILE), :]
            dconv[at(k, r), :] = norm_back(n, f_conv[pl.ds(r, TILE), 0:1], upward).astype(BF16)

        tiles(first)
        send_halos(1, k, dconv, (dconv_behind, dconv_ahead))

    def leave(k):
        rows = at(k, 0, CH)
        narrow[...] = dot_t(dconv[rows, :], taps_i[1])
        for copy in dconv_halos(k):
            copy.wait_recv()
        narrow[...] += dot_t(dconv_ahead[rows, :], taps_i[0]) + dot_t(dconv_behind[rows, :], taps_i[2])

        def first(r):
            upward = sl_mid[at(k, r), :] * narrow[pl.ds(r, TILE), :]
            ent[pl.ds(r, TILE), :BOT] = norm_back(n_mid[at(k, r), :], f_mid[at(k, r), 0:1], upward).astype(BF16)

        tiles(first)
        wide[...] = dot_t(ent[:, :BOT], sq_i[...])

        def second(r):
            upward = sl_in[at(k, r), :] * wide[pl.ds(r, TILE), :]
            back = norm_back(n_in[at(k, r), :], f_in[at(k, r), 0:1], upward)
            outs_send[at(k, r), :] = (g[at(k, r), :] + back).astype(BF16)

        tiles(second)
        for copy in turns(1, k):
            copy.start()

    def loop(count, body):
        def step(k, carry):
            body(k)
            return carry

        lax.fori_loop(0, count, step, 0)

    dec[...] = jnp.zeros_like(dec)
    dec[pl.ds(0, VOCAB), :] = decoder[...]
    pl.semaphore_wait(barrier, 5)

    def fetch(k):
        for copy in turns(0, k):
            copy.start()

    loop(CHUNKS, fetch)
    weights[0].wait()
    loop(CHUNKS, enter)
    loop(CHUNKS, prepare)
    for weight in weights[1:]:
        weight.wait()

    def middle(k):
        converse(k)
        outer(k)
        turn_back(k)

    loop(CHUNKS, middle)
    loop(CHUNKS, leave)

    def finish(k):
        for copy in mid_halos(k) + dconv_halos(k):
            copy.wait_send()
        await_turns(3, k)
        loss_out[k] = dot_t(jnp.ones((8, EXTRA), BF16), loss_back[at(k, 0, CH), :])[0:1]
        await_turns(1, k)
        for stage in range(4):
            for copy in turns(stage, k)[:3]:
                copy.wait_send()

    loop(CHUNKS, finish)


def on_device(activations, targets, sq_i, taps_i, ex_i, sq_o, taps_o, ex_o, decoder):
    anywhere = pl.BlockSpec(memory_space=pltpu.HBM)
    vmem = pl.BlockSpec(memory_space=pltpu.VMEM)
    targets = targets.reshape(CHUNKS, 1, CH)
    v = pltpu.VMEM
    dma = pltpu.SemaphoreType.DMA
    out, loss = pl.pallas_call(
        kernel,
        out_shape=(
            pltpu.VMEM((ROWS, D), BF16),
            pltpu.VMEM((CHUNKS, 1, CH), F32),
        ),
        in_specs=[anywhere, vmem, vmem] + [anywhere] * 6,
        out_specs=(vmem, vmem),
        scratch_shapes=[
            v((ROWS, D), BF16),
            v((D, BOT), BF16), v((3, BOT, BOT), BF16), v((BOT, D), BF16),
            v((D, BOT), BF16), v((3, BOT, BOT), BF16), v((BOT, D), BF16),
            v((ROWS, D), F32), v((ROWS, 128), F32),
            v((ROWS, BOT), F32), v((ROWS, 128), F32),
            v((ROWS, BOT), F32), v((ROWS, 128), F32),
            v((ROWS, D), F32), v((ROWS, BOT), F32),
            v((ROWS, BOT), BF16), v((ROWS, BOT), BF16), v((ROWS, BOT), BF16),
            v((ROWS, BOT), BF16), v((ROWS, BOT), BF16), v((ROWS, BOT), BF16),
            v((CH, D), BF16), v((ROWS, D), F32), v((ROWS, D), BF16),
            v((ROWS, EXTRA), BF16), v((ROWS, EXTRA), BF16), v((ROWS, EXTRA), BF16), v((ROWS, EXTRA), BF16),
            v((CH, D), BF16), v((CH, D), F32), v((CH, BOT), F32),
            v((CH, D), F32), v((CH, 128), F32), v((CH, BOT), F32), v((CH, 128), F32),
            v((CH, BOT), F32), v((CH, 128), F32), v((CH, D), F32),
            v((CH + 2 * QUARTER, BOT), BF16), v((CH + 2 * QUARTER, BOT), BF16), v((EXTRA, D), BF16),
            dma((6,)), dma((4, CHUNKS)),
            dma((2, 2, CHUNKS)), dma((2, 2, CHUNKS)), dma((4, 4, CHUNKS)), dma((4, 4, CHUNKS)),
        ],
        compiler_params=pltpu.CompilerParams(
            collective_id=0, has_side_effects=True, vmem_limit_bytes=62 * 1024 * 1024
        ),
    )(activations, targets, decoder, sq_i, taps_i, ex_i, sq_o, taps_o, ex_o)
    return out, loss.reshape(ROWS)


def solution(mesh):
    rows = P(("coarse", "fine"))
    return jax.shard_map(
        on_device,
        mesh=mesh,
        in_specs=(P(("coarse", "fine"), None), rows, P(), P(), P(), P(), P(), P(), P()),
        out_specs=(P(("coarse", "fine"), None), rows),
        check_vma=False,
    )
```
